32 devices in a mesh: groups: 2 (over x), tp: 16 (over z, y, core).
Axes of the slice: x: 2, y: 2, z: 4, core: 2. Of those that a mesh axis runs over, the one named last changes fastest.
Arguments:
- frames: bfloat16 [128, 1280], P(('groups', 'tp')), parts along dimension 0, may hold values from -6 to 6
- enc_gain: float32 [1280], replicated, may hold values from 0.1 to 1.9
- enc_shift: float32 [1280], replicated, may hold values from -1.75 to 1.75
- enc_up: bfloat16 [5120, 1280], P('tp'), may hold values from -0.15625 to 0.15625
- enc_up_bias: bfloat16 [5120], P('tp'), may hold values from -3 to 3
- enc_down: bfloat16 [5120, 1280], P('tp'), may hold values from -0.15625 to 0.15625
- enc_down_bias: float32 [1280], replicated, may hold values from -1.75 to 1.75
- post_gain: float32 [1280], replicated, may hold values from 0.1 to 1.9
- post_shift: float32 [1280], replicated, may hold values from -3 to 3
- proj_weight: bfloat16 [1280, 4096], P(None, 'tp'), may hold values from -0.15625 to 0.15625
- proj_bias: float32 [4096], P('tp'), may hold values from -1.75 to 1.75
- slot_source: int32 [128], P('groups'), parts along dimension 0, may hold values from -1 to 31, as said below
- prompt_embeds: bfloat16 [128, 4096], P(('groups', 'tp')), parts along dimension 0, may hold values from -6 to 6
- rms_gain: float32 [4096], replicated, may hold values from 0.1 to 1.9
- gate_weight: bfloat16 [4096, 11008], P(None, 'tp'), may hold values from -0.09375 to 0.09375
- up_weight: bfloat16 [4096, 11008], P(None, 'tp'), may hold values from -0.09375 to 0.09375
- down_weight: bfloat16 [11008, 4096], P('tp'), may hold values from -0.109375 to 0.109375
Outputs:
- prefill_out: bfloat16 [128, 4096], P(('groups', 'tp')), parts along dimension 0
The draws below stay inside these ranges and needn't reach their ends.
There are 2 independent parts, one for each index of `groups`. The reference program is written for one: setup_inputs(seed, part) draws one part's arguments, and reference() takes and returns one part's arrays. A program takes and returns all parts, laid end to end along the dimension named above; an argument that names none is the same for every part. Nothing has to cross between parts.
Inputs may be any that keep to these rules, and one draw needn't show every extreme that they name: `slot_source`: each of the 32 pooled audio rows appears exactly once; the other 32 entries are -1. The same list is known to every device.
All inputs are finite; a program needn't handle non-finite values.
Results may differ from the reference program's by a relative error of at most 0.0072.
Values may be sent and summed in bfloat16 or wider, within the bound.
No kernel may reach another device: no remote copies, remote signals or barrier semaphores. Data moves between devices by JAX's collectives and lax.ppermute only.
A program may use at most 64 MiB of HBM per device.

```python
import jax
import jax.numpy as jnp
from jax import lax

D = 4096
FF = 11008
ENC_D = 1280
ENC_FF = 5120
FRAMES = 64
AUDIO = 32
SLOTS = 64


def draw_slot_source(key, part):
    key = jax.random.fold_in(key, 11)
    order = jax.random.permutation(key, SLOTS)
    ranking = jnp.zeros((SLOTS,), jnp.int32).at[order].set(jnp.arange(SLOTS, dtype=jnp.int32))
    return jnp.where(ranking < AUDIO, ranking, -1).astype(jnp.int32)


def steps_of(key, dims, cuts, least, high):
    level = 1.0
    for dim, parts in cuts:
        heights = jax.random.uniform(jax.random.fold_in(jax.random.fold_in(key, 6), dim), (parts,), jnp.float32, least / len(cuts), high / len(cuts))
        level = level * jnp.repeat(jnp.exp(heights), dims[dim] // parts).reshape((-1,) + (1,) * (len(dims) - 1 - dim))
    return level


def scatter_about(key, dims, deviation, limit, split=(), held_as=jnp.bfloat16):
    level = steps_of(key, dims, split, -0.22, 0.18) if split else 1.0
    entries = jax.random.normal(key, dims, jnp.float32) * deviation * level
    return jnp.minimum(jnp.maximum(entries, -limit), limit).astype(held_as)


def setup_inputs(seed: int = 0, part: int = 0) -> dict:
    keys = jax.random.split(jax.random.key(seed), 18)
    part_splits = jax.random.split(jax.random.fold_in(keys[17], part), 18)
    frames = scatter_about(part_splits[0], (FRAMES, ENC_D), 1.0, 6.0, ((0, 16),))
    enc_gain = jnp.clip(1.0 + 0.18 * jax.random.normal(keys[1], (ENC_D,), jnp.float32), 0.1, 1.9)
    enc_shift = scatter_about(keys[2], (ENC_D,), 0.3, 1.75, (), jnp.float32)
    enc_up = scatter_about(keys[3], (ENC_FF, ENC_D), ENC_D ** -0.5, 0.15625, ((0, 16),))
    enc_up_bias = scatter_about(keys[4], (ENC_FF,), 0.5, 3.0, ((0, 16),))
    enc_down = scatter_about(keys[5], (ENC_FF, ENC_D), (ENC_FF // 4) ** -0.5, 0.15625, ((0, 16),))
    enc_down_bias = scatter_about(keys[6], (ENC_D,), 0.3, 1.75, (), jnp.float32)
    post_gain = jnp.clip(1.0 + 0.18 * jax.random.normal(keys[7], (ENC_D,), jnp.float32), 0.1, 1.9)
    post_shift = scatter_about(keys[8], (ENC_D,), 0.5, 3.0, (), jnp.float32)
    proj_weight = scatter_about(keys[9], (ENC_D, D), ENC_D ** -0.5, 0.15625, ((1, 16),))
    proj_bias = scatter_about(keys[10], (D,), 0.3, 1.75, ((0, 16),), jnp.float32)
    slot_source = draw_slot_source(jax.random.fold_in(jax.random.fold_in(keys[17], part), 71), part)
    prompt_embeds = scatter_about(part_splits[12], (SLOTS, D), 1.0, 6.0, ((0, 16),))
    rms_gain = jnp.clip(1.0 + 0.18 * jax.random.normal(keys[13], (D,), jnp.float32), 0.1, 1.9)
    gate_weight = scatter_about(keys[14], (D, FF), D ** -0.5, 0.09375, ((1, 16),))
    up_weight = scatter_about(keys[15], (D, FF), D ** -0.5, 0.09375, ((1, 16),))
    down_weight = scatter_about(keys[16], (FF, D), (FF // 4) ** -0.5, 0.109375, ((0, 16),))
    return {"frames": frames, "enc_gain": enc_gain, "enc_shift": enc_shift, "enc_up": enc_up, "enc_up_bias": enc_up_bias, "enc_down": enc_down, "enc_down_bias": enc_down_bias, "post_gain": post_gain, "post_shift": post_shift, "proj_weight": proj_weight, "proj_bias": proj_bias, "slot_source": slot_source, "prompt_embeds": prompt_embeds, "rms_gain": rms_gain, "gate_weight": gate_weight, "up_weight": up_weight, "down_weight": down_weight}


def layer_norm(values, gain, shift):
    center = values - lax.optimization_barrier(jnp.mean(values, axis=-1, keepdims=True))
    spread = lax.optimization_barrier(jnp.mean(center * center, axis=-1, keepdims=True))
    return center * lax.rsqrt(spread + 1e-05) * gain + shift

def reference(frames, enc_gain, enc_shift, enc_up, enc_up_bias, enc_down, enc_down_bias, post_gain, post_shift, proj_weight, proj_bias, slot_source, prompt_embeds, rms_gain, gate_weight, up_weight, down_weight):
    source = frames.astype(jnp.float32)
    enc_normed = layer_norm(source, enc_gain, enc_shift).astype(jnp.bfloat16)
    pre_act = jnp.dot(enc_normed, enc_up.T, preferred_element_type=jnp.float32) + enc_up_bias.astype(jnp.float32)
    enc_hidden = jax.nn.gelu(pre_act, approximate=False).astype(jnp.bfloat16)
    enc_out = source + jnp.dot(enc_hidden, enc_down, preferred_element_type=jnp.float32) + enc_down_bias
    paired = enc_out.reshape(AUDIO, 2, ENC_D)
    pooled = (paired[:, 0, :] + paired[:, 1, :]) * 0.5
    post = layer_norm(pooled, post_gain, post_shift).astype(jnp.bfloat16)
    projected = (jnp.dot(post, proj_weight, preferred_element_type=jnp.float32) + proj_bias).astype(jnp.bfloat16)
    clipped = jnp.maximum(slot_source, 0).astype(jnp.int32)
    packed = jnp.where((slot_source >= 0)[:, None], jnp.take(projected, clipped, axis=0), prompt_embeds)
    residual = packed.astype(jnp.float32)
    scale = lax.rsqrt(lax.optimization_barrier(jnp.mean(residual * residual, axis=-1, keepdims=True)) + 1e-06)
    lm_normed = (residual * scale * rms_gain).astype(jnp.bfloat16)
    gate = jnp.dot(lm_normed, gate_weight, preferred_element_type=jnp.float32)
    lifted = jnp.dot(lm_normed, up_weight, preferred_element_type=jnp.float32)
    lm_hidden = (jax.nn.silu(gate) * lifted).astype(jnp.bfloat16)
    return (residual + jnp.dot(lm_hidden, down_weight, preferred_element_type=jnp.float32)).astype(jnp.bfloat16)
```

```python
import jax
import jax.numpy as jnp
from jax import lax
from jax.sharding import PartitionSpec as P


def layer_norm(values, gain, shift):
    center = values - jnp.mean(values, axis=-1, keepdims=True)
    spread = jnp.mean(center * center, axis=-1, keepdims=True)
    return center * lax.rsqrt(spread + 1e-05) * gain + shift


def to_every(piece, count):
    spread = jnp.broadcast_to(piece[None], (count,) + piece.shape)
    return lax.all_to_all(spread, "tp", 0, 0)


def reduce_rows(partial_value, count):
    rows, width = partial_value.shape
    pieces = partial_value.astype(jnp.bfloat16).reshape(count, rows // count, width)
    return jnp.sum(lax.all_to_all(pieces, "tp", 0, 0).astype(jnp.float32), axis=0)


def pool(values):
    paired = values.reshape(values.shape[0] // 2, 2, values.shape[1])
    return (paired[:, 0, :] + paired[:, 1, :]) * 0.5


def shards(
    frames,
    enc_gain,
    enc_shift,
    enc_up,
    enc_up_bias,
    enc_down,
    enc_down_bias,
    post_gain,
    post_shift,
    proj_weight,
    proj_bias,
    slot_source,
    prompt_embeds,
    rms_gain,
    gate_weight,
    up_weight,
    down_weight,
):
    count = lax.axis_size("tp")
    me = lax.axis_index("tp")
    gathered = to_every(frames, count).reshape(-1, frames.shape[1])
    prompts = to_every(prompt_embeds, count).reshape(-1, prompt_embeds.shape[1])
    normed = layer_norm(gathered.astype(jnp.float32), enc_gain, enc_shift).astype(jnp.bfloat16)
    pre_act = lax.dot_general(
        normed, enc_up, (((1,), (1,)), ((), ())), preferred_element_type=jnp.float32
    )
    hidden = jax.nn.gelu(pre_act + enc_up_bias.astype(jnp.float32), approximate=False)
    partial_value = jnp.dot(
        hidden.astype(jnp.bfloat16), enc_down, preferred_element_type=jnp.float32
    )
    branch = reduce_rows(pool(partial_value), count)
    pooled = pool(frames.astype(jnp.float32)) + branch + enc_down_bias
    post = layer_norm(pooled, post_gain, post_shift).astype(jnp.bfloat16)
    post_every = to_every(post, count).reshape(-1, post.shape[1])
    projected = (
        jnp.dot(post_every, proj_weight, preferred_element_type=jnp.float32) + proj_bias
    ).astype(jnp.bfloat16)
    features = to_every(projected, count)
    features = jnp.transpose(features, (1, 0, 2)).reshape(projected.shape[0], -1)
    clipped = jnp.maximum(slot_source, 0)
    packed = jnp.where(
        (slot_source >= 0)[:, None], jnp.take(features, clipped, axis=0), prompts
    )
    residual = packed.astype(jnp.float32)
    scale = lax.rsqrt(jnp.mean(residual * residual, axis=-1, keepdims=True) + 1e-06)
    lm_normed = (residual * scale * rms_gain).astype(jnp.bfloat16)
    gate = jnp.dot(lm_normed, gate_weight, preferred_element_type=jnp.float32)
    lifted = jnp.dot(lm_normed, up_weight, preferred_element_type=jnp.float32)
    lm_hidden = (jax.nn.silu(gate) * lifted).astype(jnp.bfloat16)
    summed = reduce_rows(
        jnp.dot(lm_hidden, down_weight, preferred_element_type=jnp.float32), count
    )
    row_count = prompt_embeds.shape[0]
    own = lax.dynamic_slice_in_dim(packed, me * row_count, row_count).astype(jnp.float32)
    return (own + summed).astype(jnp.bfloat16)


def solution(mesh):
    placed = (
        P(("groups", "tp"), None),
        P(),
        P(),
        P("tp", None),
        P("tp"),
        P("tp", None),
        P(),
        P(),
        P(),
        P(None, "tp"),
        P("tp"),
        P("groups"),
        P(("groups", "tp"), None),
        P(),
        P(None, "tp"),
        P(None, "tp"),
        P("tp", None),
    )
    return jax.shard_map(
        shards, mesh=mesh, in_specs=placed, out_specs=P(("groups", "tp"), None), check_vma=False
    )
```

```python
import functools

import jax
import jax.numpy as jnp
from jax import lax
from jax.experimental import pallas as pl
from jax.experimental.pallas import tpu as pltpu
from jax.sharding import PartitionSpec as P


def mask_of(bit):
    return (1 << bit) | 1 if bit else 1


def slot_of(offset, bits):
    parity = offset & 1
    slot = 0
    for bit in range(1, bits):
        one = (offset >> bit) & 1
        parity = parity ^ one
        slot = slot + (one << (bits - 1 - bit))
    return slot + (parity << (bits - 1))


def offset_of(slot, bits):
    offset = (slot >> (bits - 1)) & 1
    for bit in range(1, bits):
        offset = offset ^ (((slot >> (bits - 1 - bit)) & 1) * mask_of(bit))
    return offset


def swap(value, bit, count):
    pairs = [(i, i ^ mask_of(bit)) for i in range(count)]
    return lax.ppermute(value, "tp", pairs)


def gather_slots(value, bits):
    for bit in list(range(bits - 1, 0, -1)) + [0]:
        value = jnp.concatenate([value, swap(value, bit, 1 << bits)], axis=0)
    return value


def in_hbm(value):
    return pltpu.with_memory_space_constraint(value, pltpu.HBM)


def row(ref, part=slice(None)):
    return ref[part].reshape(1, -1)


def dot_last(left, right):
    return lax.dot_general(
        left, right, (((1,), (1,)), ((), ())), preferred_element_type=jnp.float32
    )


def encoder_kernel(
    bits, me_ref, frames, gain, shift, bias, down_bias, up_hbm, down_hbm, gate_hbm,
    send, keep, base, gate, up, down, sems,
):
    copies = [
        pltpu.make_async_copy(source, target, sems.at[i])
        for i, (source, target) in enumerate(((up_hbm, up), (down_hbm, down), (gate_hbm, gate)))
    ]
    for copy in copies:
        copy.start()
    me = me_ref[0]
    rows, width = frames.shape
    pooled = rows // 2
    half = pooled // 2
    own = rows >> bits
    out_row = lax.broadcasted_iota(jnp.int32, (rows, rows), 0)
    in_row = lax.broadcasted_iota(jnp.int32, (rows, rows), 1)
    frame = jnp.where(out_row < pooled, 2 * out_row, 2 * (out_row - pooled) + 1)
    place = slot_of((frame // own) ^ me, bits) * own + frame % own
    order = jnp.where(place == in_row, 1.0, 0.0).astype(jnp.bfloat16)
    values = jnp.dot(order, frames[...], preferred_element_type=jnp.float32)
    both = (values[:pooled] + values[pooled:]) * 0.5 + row(down_bias)
    center = values - jnp.mean(values, axis=-1, keepdims=True)
    spread = jnp.mean(center * center, axis=-1, keepdims=True)
    normed = (center * lax.rsqrt(spread + 1e-05) * row(gain) + row(shift)).astype(jnp.bfloat16)
    copies[0].wait()
    pre_act = dot_last(normed, up[...]) + row(bias).astype(jnp.float32)
    hidden = (0.5 * pre_act * (1.0 + lax.erf(pre_act * 0.7071067811865476))).astype(jnp.bfloat16)
    copies[1].wait()
    result = jnp.dot(hidden, down[...], preferred_element_type=jnp.float32)
    mine = (result[:pooled] + result[pooled:]) * 0.5
    parity = me
    for bit in range(1, bits):
        parity = parity ^ (me >> bit)
    upper = (parity & 1) == 1
    keep[...] = jnp.where(upper, mine[half:], mine[:half])
    send[...] = jnp.where(upper, mine[:half], mine[half:]).astype(jnp.bfloat16)
    base[...] = jnp.where(upper, both[half:], both[:half])
    copies[2].wait()


def encoder(me, frames, gain, shift, bias, down_bias, up, down, gate, bits):
    rows, width = frames.shape
    half = rows // 4
    vmem = pl.BlockSpec(memory_space=pltpu.VMEM)
    hbm = pl.BlockSpec(memory_space=pltpu.HBM)
    return pl.pallas_call(
        functools.partial(encoder_kernel, bits),
        out_shape=[
            jax.ShapeDtypeStruct((half, width), jnp.bfloat16),
            jax.ShapeDtypeStruct((half, width), jnp.float32),
            jax.ShapeDtypeStruct((half, width), jnp.float32),
            pltpu.VMEM(gate.shape, gate.dtype),
        ],
        in_specs=[pl.BlockSpec(memory_space=pltpu.SMEM)] + [vmem] * 5 + [hbm] * 3,
        out_specs=[vmem] * 4,
        scratch_shapes=[
            pltpu.VMEM(up.shape, up.dtype),
            pltpu.VMEM(down.shape, down.dtype),
            pltpu.SemaphoreType.DMA((3,)),
        ],
        compiler_params=pltpu.CompilerParams(vmem_limit_bytes=12 * 2**20),
        cost_estimate=pl.CostEstimate(
            flops=4 * rows * up.size, bytes_accessed=4 * up.size + 2 * gate.size, transcendentals=0
        ),
    )(me, frames, gain, shift, bias, down_bias, in_hbm(up), in_hbm(down), in_hbm(gate))


def language_kernel(
    bits, pieces, me_ref, features, source, prompts, gain, gate, up_hbm, down_hbm,
    send, keep, packed, up, down, sems,
):
    count, audio, columns = features.shape
    rows, width = prompts.shape
    half = rows // 2
    own = rows >> bits
    span = width // pieces
    parts = [slice(i * span, (i + 1) * span) for i in range(pieces)]
    ups = [
        pltpu.make_async_copy(
            up_hbm.at[:, pl.ds(i * span, span)], up.at[:, pl.ds(i * span, span)], sems.at[i]
        )
        for i in range(pieces)
    ]
    downs = [
        pltpu.make_async_copy(
            down_hbm.at[:, pl.ds(i * span, span)],
            down.at[:, pl.ds(i * span, span)],
            sems.at[pieces + i],
        )
        for i in range(pieces)
    ]
    for copy in ups + downs:
        copy.start()
    me = me_ref[0]
    out_row = lax.broadcasted_iota(jnp.int32, (rows, rows), 0)
    in_row = lax.broadcasted_iota(jnp.int32, (rows, rows), 1)
    place = (offset_of(out_row // own, bits) ^ me) * own + out_row % own
    order = jnp.where(place == in_row, 1.0, 0.0).astype(jnp.bfloat16)
    wanted = lax.broadcasted_iota(jnp.int32, (audio, rows), 0)
    chosen = jnp.where(row(source) == wanted, 1.0, 0.0).astype(jnp.bfloat16)
    pick = dot_last(order, chosen)
    audio_row = jnp.sum(pick, axis=1, keepdims=True) > 0.5
    pick = pick.astype(jnp.bfloat16)
    squares = jnp.zeros((rows, columns), jnp.float32)
    for device in range(count):
        part = slice(device * columns, (device + 1) * columns)
        found = jnp.dot(
            pick, features[slot_of(me ^ device, bits)], preferred_element_type=jnp.float32
        )
        value = jnp.where(audio_row, found, prompts[:, part].astype(jnp.float32))
        squares += value * value
        packed[:, part] = value.astype(jnp.bfloat16)
    scale = lax.rsqrt(jnp.sum(squares, axis=1, keepdims=True) / width + 1e-06)

    def normed(part):
        return (packed[:, part].astype(jnp.float32) * scale * row(gain, part)).astype(jnp.bfloat16)

    gated = sum(dot_last(normed(part), gate[:, part]) for part in parts)
    lifted = 0.0
    for part, copy in zip(parts, ups):
        copy.wait()
        lifted += dot_last(normed(part), up[:, part])
    hidden = (gated * jax.nn.sigmoid(gated) * lifted).astype(jnp.bfloat16)
    held = lax.broadcasted_iota(jnp.int32, (half, 1), 0) < own
    for part, copy in zip(parts, downs):
        copy.wait()
        result = jnp.dot(hidden, down[:, part], preferred_element_type=jnp.float32)
        send[:, part] = result[half:].astype(jnp.bfloat16)
        keep[:, part] = result[:half] + jnp.where(
            held, packed[:half, part].astype(jnp.float32), 0.0
        )


def language(me, features, source, prompts, gain, gate, up, down, bits):
    rows, width = prompts.shape
    pieces = 4
    vmem = pl.BlockSpec(memory_space=pltpu.VMEM)
    hbm = pl.BlockSpec(memory_space=pltpu.HBM)
    return pl.pallas_call(
        functools.partial(language_kernel, bits, pieces),
        out_shape=[
            jax.ShapeDtypeStruct((rows // 2, width), jnp.bfloat16),
            jax.ShapeDtypeStruct((rows // 2, width), jnp.float32),
        ],
        in_specs=[pl.BlockSpec(memory_space=pltpu.SMEM)] + [vmem] * 5 + [hbm] * 2,
        out_specs=[vmem] * 2,
        scratch_shapes=[
            pltpu.VMEM((rows, width), jnp.bfloat16),
            pltpu.VMEM(up.shape, up.dtype),
            pltpu.VMEM(down.shape, down.dtype),
            pltpu.SemaphoreType.DMA((2 * pieces,)),
        ],
        compiler_params=pltpu.CompilerParams(vmem_limit_bytes=24 * 2**20),
        cost_estimate=pl.CostEstimate(
            flops=6 * rows * up.size, bytes_accessed=4 * up.size, transcendentals=0
        ),
    )(me, features, source, prompts, gain, gate, in_hbm(up), in_hbm(down))


def layer_norm(values, gain, shift):
    center = values - jnp.mean(values, axis=-1, keepdims=True)
    spread = jnp.mean(center * center, axis=-1, keepdims=True)
    return center * lax.rsqrt(spread + 1e-05) * gain + shift


def to_every(piece, count):
    spread = jnp.broadcast_to(piece[None], (count,) + piece.shape)
    return lax.all_to_all(spread, "tp", 0, 0)


def reduce_rows(partial_value, count):
    rows, width = partial_value.shape
    pieces = partial_value.astype(jnp.bfloat16).reshape(count, rows // count, width)
    return jnp.sum(lax.all_to_all(pieces, "tp", 0, 0).astype(jnp.float32), axis=0)


def pool(values):
    paired = values.reshape(values.shape[0] // 2, 2, values.shape[1])
    return (paired[:, 0, :] + paired[:, 1, :]) * 0.5


def shards(
    frames,
    enc_gain,
    enc_shift,
    enc_up,
    enc_up_bias,
    enc_down,
    enc_down_bias,
    post_gain,
    post_shift,
    proj_weight,
    proj_bias,
    slot_source,
    prompt_embeds,
    rms_gain,
    gate_weight,
    up_weight,
    down_weight,
):
    count = lax.axis_size("tp")
    me = lax.axis_index("tp")
    gathered = to_every(frames, count).reshape(-1, frames.shape[1])
    prompts = to_every(prompt_embeds, count).reshape(-1, prompt_embeds.shape[1])
    normed = layer_norm(gathered.astype(jnp.float32), enc_gain, enc_shift).astype(jnp.bfloat16)
    pre_act = lax.dot_general(
        normed, enc_up, (((1,), (1,)), ((), ())), preferred_element_type=jnp.float32
    )
    hidden = jax.nn.gelu(pre_act + enc_up_bias.astype(jnp.float32), approximate=False)
    partial_value = jnp.dot(
        hidden.astype(jnp.bfloat16), enc_down, preferred_element_type=jnp.float32
    )
    branch = reduce_rows(pool(partial_value), count)
    pooled = pool(frames.astype(jnp.float32)) + branch + enc_down_bias
    post = layer_norm(pooled, post_gain, post_shift).astype(jnp.bfloat16)
    post_every = to_every(post, count).reshape(-1, post.shape[1])
    projected = (
        jnp.dot(post_every, proj_weight, preferred_element_type=jnp.float32) + proj_bias
    ).astype(jnp.bfloat16)
    features = to_every(projected, count)
    features = jnp.transpose(features, (1, 0, 2)).reshape(projected.shape[0], -1)
    clipped = jnp.maximum(slot_source, 0)
    packed = jnp.where(
        (slot_source >= 0)[:, None], jnp.take(features, clipped, axis=0), prompts
    )
    residual = packed.astype(jnp.float32)
    scale = lax.rsqrt(jnp.mean(residual * residual, axis=-1, keepdims=True) + 1e-06)
    lm_normed = (residual * scale * rms_gain).astype(jnp.bfloat16)
    gate = jnp.dot(lm_normed, gate_weight, preferred_element_type=jnp.float32)
    lifted = jnp.dot(lm_normed, up_weight, preferred_element_type=jnp.float32)
    lm_hidden = (jax.nn.silu(gate) * lifted).astype(jnp.bfloat16)
    summed = reduce_rows(
        jnp.dot(lm_hidden, down_weight, preferred_element_type=jnp.float32), count
    )
    row_count = prompt_embeds.shape[0]
    own = lax.dynamic_slice_in_dim(packed, me * row_count, row_count).astype(jnp.float32)
    return (own + summed).astype(jnp.bfloat16)


def fused_shards(
    bits,
    frames,
    enc_gain,
    enc_shift,
    enc_up,
    enc_up_bias,
    enc_down,
    enc_down_bias,
    post_gain,
    post_shift,
    proj_weight,
    proj_bias,
    slot_source,
    prompt_embeds,
    rms_gain,
    gate_weight,
    up_weight,
    down_weight,
):
    count = 1 << bits
    index = lax.axis_index("tp")
    me = index.reshape(1).astype(jnp.int32)
    gathered = gather_slots(frames, bits)
    prompts = gather_slots(prompt_embeds, bits)
    send, total, base, gate = encoder(
        me,
        gathered,
        enc_gain,
        enc_shift,
        enc_up_bias,
        enc_down_bias,
        enc_up,
        enc_down,
        gate_weight.T,
        bits,
    )
    total = total + swap(send, 0, count).astype(jnp.float32)
    for bit in range(1, bits):
        total = total + swap(total.astype(jnp.bfloat16), bit, count).astype(jnp.float32)
    post = layer_norm(total + base, post_gain, post_shift).astype(jnp.bfloat16)
    other = swap(post, 0, count)
    parity = index
    for bit in range(1, bits):
        parity = parity ^ (index >> bit)
    upper = (parity & 1) == 1
    post_every = jnp.where(
        upper, jnp.concatenate([other, post]), jnp.concatenate([post, other])
    )
    projected = (
        jnp.dot(post_every, proj_weight, preferred_element_type=jnp.float32) + proj_bias
    ).astype(jnp.bfloat16)
    features = gather_slots(projected[None], bits)
    send, total = language(
        me,
        features,
        slot_source,
        prompts,
        rms_gain,
        gate,
        up_weight.T,
        down_weight,
        bits,
    )
    total = total + swap(send, 0, count).astype(jnp.float32)
    for bit in range(1, bits):
        half = total.shape[0] // 2
        arrived = swap(total[half:].astype(jnp.bfloat16), bit, count)
        total = total[:half] + arrived.astype(jnp.float32)
    return total.astype(jnp.bfloat16)


def any_shards(*arrays):
    count = lax.axis_size("tp")
    bits = count.bit_length() - 1
    whole_tiles = (
        arrays[9].shape[1] % 128 == 0
        and arrays[3].shape[0] % 16 == 0
        and arrays[16].shape[0] % 16 == 0
    )
    if count == 1 << bits and bits > 1 and whole_tiles:
        return fused_shards(bits, *arrays)
    return shards(*arrays)


def solution(mesh):
    placed = (
        P(("groups", "tp"), None),
        P(),
        P(),
        P("tp", None),
        P("tp"),
        P("tp", None),
        P(),
        P(),
        P(),
        P(None, "tp"),
        P("tp"),
        P("groups"),
        P(("groups", "tp"), None),
        P(),
        P(None, "tp"),
        P(None, "tp"),
        P("tp", None),
    )
    return jax.shard_map(
        any_shards, mesh=mesh, in_specs=placed, out_specs=P(("groups", "tp"), None), check_vma=False
    )
```

```python
import functools

import jax
import jax.numpy as jnp
from jax import lax
from jax.experimental import pallas as pl
from jax.experimental.pallas import tpu as pltpu
from jax.sharding import PartitionSpec as P


def mask_of(bit):
    return (1 << bit) | 1 if bit else 1


def slot_of(offset, bits):
    parity = offset & 1
    slot = 0
    for bit in range(1, bits):
        one = (offset >> bit) & 1
        parity = parity ^ one
        slot = slot + (one << (bits - 1 - bit))
    return slot + (parity << (bits - 1))


def offset_of(slot, bits):
    offset = (slot >> (bits - 1)) & 1
    for bit in range(1, bits):
        offset = offset ^ (((slot >> (bits - 1 - bit)) & 1) * mask_of(bit))
    return offset


def swap(value, bit, count):
    pairs = [(i, i ^ mask_of(bit)) for i in range(count)]
    return lax.ppermute(value, "tp", pairs)


def parity_of(index, bits):
    parity = index
    for bit in range(1, bits):
        parity = parity ^ (index >> bit)
    return parity & 1


def in_hbm(value):
    return pltpu.with_memory_space_constraint(value, pltpu.HBM)


def row(ref, part=slice(None)):
    return ref[part].reshape(1, -1)


def dot_last(left, right):
    return lax.dot_general(
        left, right, (((1,), (1,)), ((), ())), preferred_element_type=jnp.float32
    )


def encoder_kernel(
    bits, frames, others, gain, shift, down_bias, bias, up, down, send, keep, base
):
    me = lax.axis_index("tp")
    first = frames.shape[0]
    rows = 2 * first
    pooled = rows // 2
    half = pooled // 2
    own = rows >> bits
    out_row = lax.broadcasted_iota(jnp.int32, (rows, rows), 0)
    in_row = lax.broadcasted_iota(jnp.int32, (rows, rows), 1)
    frame = jnp.where(out_row < pooled, 2 * out_row, 2 * (out_row - pooled) + 1)
    place = slot_of((frame // own) ^ me, bits) * own + frame % own
    order = jnp.where(place == in_row, 1.0, 0.0).astype(jnp.bfloat16)
    values = jnp.dot(
        order, jnp.concatenate([frames[...], others[...]]), preferred_element_type=jnp.float32
    )
    center = values - jnp.mean(values, axis=-1, keepdims=True)
    spread = jnp.mean(center * center, axis=-1, keepdims=True)
    both = (values[:pooled] + values[pooled:]) * 0.5 + row(down_bias)
    normed = (center * lax.rsqrt(spread + 1e-05) * row(gain) + row(shift)).astype(jnp.bfloat16)
    pre_act = dot_last(normed, up[...]) + row(bias).astype(jnp.float32)
    hidden = (0.5 * pre_act * (1.0 + lax.erf(pre_act * 0.7071067811865476))).astype(jnp.bfloat16)
    result = jnp.dot(hidden, down[...], preferred_element_type=jnp.float32)
    mine = (result[:pooled] + result[pooled:]) * 0.5
    upper = parity_of(me, bits) == 1
    keep[...] = jnp.where(upper, mine[half:], mine[:half])
    send[...] = jnp.where(upper, mine[:half], mine[half:]).astype(jnp.bfloat16)
    base[...] = jnp.where(upper, both[half:], both[:half])


def encoder(halves, vectors, up, down, bits):
    first, width = halves[0].shape
    half = first // 2
    vmem = pl.BlockSpec(memory_space=pltpu.VMEM)
    return pl.pallas_call(
        functools.partial(encoder_kernel, bits),
        out_shape=[
            jax.ShapeDtypeStruct((half, width), jnp.bfloat16),
            jax.ShapeDtypeStruct((half, width), jnp.float32),
            jax.ShapeDtypeStruct((half, width), jnp.float32),
        ],
        in_specs=[vmem] * 8,
        out_specs=[vmem] * 3,
        compiler_params=pltpu.CompilerParams(vmem_limit_bytes=8 * 2**20),
        cost_estimate=pl.CostEstimate(
            flops=8 * first * up.size, bytes_accessed=4 * up.size, transcendentals=0
        ),
    )(*halves, *vectors, up, down)


def post_kernel(total, arrived, base, gain, shift, after, post):
    values = total[...] + arrived[...].astype(jnp.float32) + base[...]
    center = values - jnp.mean(values, axis=-1, keepdims=True)
    spread = jnp.mean(center * center, axis=-1, keepdims=True)
    normed = center * lax.rsqrt(spread + 1e-05) * row(gain) + row(shift)
    post[...] = normed.astype(post.dtype)


def post_norm(total, arrived, base, gain, shift, after):
    vmem = pl.BlockSpec(memory_space=pltpu.VMEM)
    return pl.pallas_call(
        post_kernel,
        out_shape=jax.ShapeDtypeStruct(total.shape, jnp.bfloat16),
        in_specs=[vmem] * 5 + [pl.BlockSpec(memory_space=pl.ANY)],
        out_specs=vmem,
        compiler_params=pltpu.CompilerParams(vmem_limit_bytes=4 * 2**20),
    )(total, arrived, base, gain, shift, after)


def project_kernel(bits, post, other, weight, bias, out):
    upper = parity_of(lax.axis_index("tp"), bits) == 1
    low = jnp.where(upper, other[...], post[...])
    high = jnp.where(upper, post[...], other[...])
    every = jnp.concatenate([low, high])
    result = jnp.dot(every, weight[...], preferred_element_type=jnp.float32) + row(bias)
    out[0] = result.astype(out.dtype)


def project(post, other, weight, bias, bits):
    vmem = pl.BlockSpec(memory_space=pltpu.VMEM)
    return pl.pallas_call(
        functools.partial(project_kernel, bits),
        out_shape=jax.ShapeDtypeStruct((1, 2 * post.shape[0], weight.shape[1]), jnp.bfloat16),
        in_specs=[vmem] * 4,
        out_specs=vmem,
        compiler_params=pltpu.CompilerParams(vmem_limit_bytes=4 * 2**20),
    )(post, other, weight, bias)


def stage_kernel(count, *refs):
    sems = refs[2 * count]
    copies = [
        pltpu.make_async_copy(refs[i], refs[count + i], sems.at[i]) for i in range(count)
    ]
    for copy in copies:
        copy.start()
    for copy in copies:
        copy.wait()


def stage(*values):
    count = len(values)
    return pl.pallas_call(
        functools.partial(stage_kernel, count),
        out_shape=[pltpu.VMEM(value.shape, value.dtype) for value in values],
        in_specs=[pl.BlockSpec(memory_space=pltpu.HBM)] * count,
        out_specs=[pl.BlockSpec(memory_space=pltpu.VMEM)] * count,
        scratch_shapes=[pltpu.SemaphoreType.DMA((count,))],
        compiler_params=pltpu.CompilerParams(vmem_limit_bytes=2 * 2**20),
    )(*[in_hbm(value) for value in values])


def fetch_kernel(start, carried, after, source, target, passed, sem):
    width = target.shape[1]
    copy = pltpu.make_async_copy(source.at[:, pl.ds(start, width)], target, sem)
    copy.start()
    passed[...] = carried[...]
    copy.wait()


def fetch(carried, after, weight, start, width):
    vmem = pl.BlockSpec(memory_space=pltpu.VMEM)
    return pl.pallas_call(
        functools.partial(fetch_kernel, start),
        out_shape=[
            pltpu.VMEM((weight.shape[0], width), weight.dtype),
            jax.ShapeDtypeStruct(carried.shape, carried.dtype),
        ],
        in_specs=[
            vmem,
            pl.BlockSpec(memory_space=pl.ANY),
            pl.BlockSpec(memory_space=pltpu.HBM),
        ],
        out_specs=[vmem] * 2,
        scratch_shapes=[pltpu.SemaphoreType.DMA],
        compiler_params=pltpu.CompilerParams(vmem_limit_bytes=2 * 2**20),
        cost_estimate=pl.CostEstimate(
            flops=0, bytes_accessed=2 * weight.shape[0] * width, transcendentals=0
        ),
    )(carried, after, in_hbm(weight))


def language_kernel(
    bits, near, far, source, prompts, others, gain, gate, rest, up, down,
    send, keep, packed, normed,
):
    count, audio, columns = near.shape
    count = 2 * count
    half, width = prompts.shape
    rows = 2 * half
    own = rows >> bits
    me = lax.axis_index("tp")
    out_row = lax.broadcasted_iota(jnp.int32, (rows, rows), 0)
    in_row = lax.broadcasted_iota(jnp.int32, (rows, rows), 1)
    place = (offset_of(out_row // own, bits) ^ me) * own + out_row % own
    order = jnp.where(place == in_row, 1.0, 0.0).astype(jnp.bfloat16)
    wanted = lax.broadcasted_iota(jnp.int32, (audio, rows), 0)
    chosen = jnp.where(row(source) == wanted, 1.0, 0.0).astype(jnp.bfloat16)
    pick = dot_last(order, chosen)
    audio_row = jnp.sum(pick, axis=1, keepdims=True) > 0.5
    pick = pick.astype(jnp.bfloat16)
    squares = jnp.zeros((rows, columns), jnp.float32)
    for device in range(count):
        part = slice(device * columns, (device + 1) * columns)
        slot = slot_of(me ^ device, bits)
        place = slot & (count // 2 - 1)
        piece = jnp.where(slot < count // 2, near[place], far[place])
        found = jnp.dot(pick, piece, preferred_element_type=jnp.float32)
        prompt = jnp.concatenate([prompts[:, part], others[:, part]])
        value = jnp.where(audio_row, found, prompt.astype(jnp.float32))
        squares += value * value
        packed[:, part] = value.astype(jnp.bfloat16)
    scale = lax.rsqrt(jnp.sum(squares, axis=1, keepdims=True) / width + 1e-06)
    for device in range(count):
        part = slice(device * columns, (device + 1) * columns)
        value = packed[:, part].astype(jnp.float32) * scale * row(gain, part)
        normed[:, part] = value.astype(jnp.bfloat16)
    cut = width // 2
    gated = dot_last(normed[:, :cut], gate[...]) + dot_last(normed[:, cut:], rest[...])
    lifted = dot_last(normed[...], up[...])
    hidden = (gated * jax.nn.sigmoid(gated) * lifted).astype(jnp.bfloat16)
    held = lax.broadcasted_iota(jnp.int32, (half, 1), 0) < own
    pieces = 4
    for piece in range(pieces):
        part = slice(piece * width // pieces, (piece + 1) * width // pieces)
        result = jnp.dot(hidden, down[:, part], preferred_element_type=jnp.float32)
        send[:, part] = result[half:].astype(jnp.bfloat16)
        keep[:, part] = result[:half] + jnp.where(
            held, packed[:half, part].astype(jnp.float32), 0.0
        )


def language(features, source, prompts, gain, gate, rest, up, down, bits):
    half, width = prompts[0].shape
    vmem = pl.BlockSpec(memory_space=pltpu.VMEM)
    return pl.pallas_call(
        functools.partial(language_kernel, bits),
        out_shape=[
            jax.ShapeDtypeStruct((half, width), jnp.bfloat16),
            jax.ShapeDtypeStruct((half, width), jnp.float32),
        ],
        in_specs=[vmem] * 10,
        out_specs=[vmem] * 2,
        scratch_shapes=[pltpu.VMEM((2 * half, width), jnp.bfloat16)] * 2,
        compiler_params=pltpu.CompilerParams(vmem_limit_bytes=12 * 2**20),
        cost_estimate=pl.CostEstimate(
            flops=12 * half * up.size, bytes_accessed=4 * up.size, transcendentals=0
        ),
    )(*features, source, *prompts, gain, gate, rest, up, down)


def layer_norm(values, gain, shift):
    center = values - jnp.mean(values, axis=-1, keepdims=True)
    spread = jnp.mean(center * center, axis=-1, keepdims=True)
    return center * lax.rsqrt(spread + 1e-05) * gain + shift


def to_every(piece, count):
    spread = jnp.broadcast_to(piece[None], (count,) + piece.shape)
    return lax.all_to_all(spread, "tp", 0, 0)


def reduce_rows(partial_value, count):
    rows, width = partial_value.shape
    pieces = partial_value.astype(jnp.bfloat16).reshape(count, rows // count, width)
    return jnp.sum(lax.all_to_all(pieces, "tp", 0, 0).astype(jnp.float32), axis=0)


def pool(values):
    paired = values.reshape(values.shape[0] // 2, 2, values.shape[1])
    return (paired[:, 0, :] + paired[:, 1, :]) * 0.5


def shards(
    frames,
    enc_gain,
    enc_shift,
    enc_up,
    enc_up_bias,
    enc_down,
    enc_down_bias,
    post_gain,
    post_shift,
    proj_weight,
    proj_bias,
    slot_source,
    prompt_embeds,
    rms_gain,
    gate_weight,
    up_weight,
    down_weight,
):
    count = lax.axis_size("tp")
    me = lax.axis_index("tp")
    gathered = to_every(frames, count).reshape(-1, frames.shape[1])
    prompts = to_every(prompt_embeds, count).reshape(-1, prompt_embeds.shape[1])
    normed = layer_norm(gathered.astype(jnp.float32), enc_gain, enc_shift).astype(jnp.bfloat16)
    pre_act = lax.dot_general(
        normed, enc_up, (((1,), (1,)), ((), ())), preferred_element_type=jnp.float32
    )
    hidden = jax.nn.gelu(pre_act + enc_up_bias.astype(jnp.float32), approximate=False)
    partial_value = jnp.dot(
        hidden.astype(jnp.bfloat16), enc_down, preferred_element_type=jnp.float32
    )
    branch = reduce_rows(pool(partial_value), count)
    pooled = pool(frames.astype(jnp.float32)) + branch + enc_down_bias
    post = layer_norm(pooled, post_gain, post_shift).astype(jnp.bfloat16)
    post_every = to_every(post, count).reshape(-1, post.shape[1])
    projected = (
        jnp.dot(post_every, proj_weight, preferred_element_type=jnp.float32) + proj_bias
    ).astype(jnp.bfloat16)
    features = to_every(projected, count)
    features = jnp.transpose(features, (1, 0, 2)).reshape(projected.shape[0], -1)
    clipped = jnp.maximum(slot_source, 0)
    packed = jnp.where(
        (slot_source >= 0)[:, None], jnp.take(features, clipped, axis=0), prompts
    )
    residual = packed.astype(jnp.float32)
    scale = lax.rsqrt(jnp.mean(residual * residual, axis=-1, keepdims=True) + 1e-06)
    lm_normed = (residual * scale * rms_gain).astype(jnp.bfloat16)
    gate = jnp.dot(lm_normed, gate_weight, preferred_element_type=jnp.float32)
    lifted = jnp.dot(lm_normed, up_weight, preferred_element_type=jnp.float32)
    lm_hidden = (jax.nn.silu(gate) * lifted).astype(jnp.bfloat16)
    summed = reduce_rows(
        jnp.dot(lm_hidden, down_weight, preferred_element_type=jnp.float32), count
    )
    row_count = prompt_embeds.shape[0]
    own = lax.dynamic_slice_in_dim(packed, me * row_count, row_count).astype(jnp.float32)
    return (own + summed).astype(jnp.bfloat16)


def fused_shards(
    bits,
    frames,
    enc_gain,
    enc_shift,
    enc_up,
    enc_up_bias,
    enc_down,
    enc_down_bias,
    post_gain,
    post_shift,
    proj_weight,
    proj_bias,
    slot_source,
    prompt_embeds,
    rms_gain,
    gate_weight,
    up_weight,
    down_weight,
):
    count = 1 << bits
    width = prompt_embeds.shape[1]
    steps = range(bits - 1, 0, -1)
    gate_rows, up_rows = gate_weight.T, up_weight.T
    arrived = swap(frames, bits - 1, count)
    (
        block, prompts, enc_gain, enc_shift, enc_down_bias, enc_up_bias, enc_up, enc_down,
        post_gain, post_shift, proj_weight, proj_bias, rms_gain, slot_source,
    ) = stage(
        frames, prompt_embeds, enc_gain, enc_shift, enc_down_bias, enc_up_bias, enc_up, enc_down,
        post_gain, post_shift, proj_weight, proj_bias, rms_gain, slot_source,
    )
    gate = []
    block = jnp.concatenate([block, arrived])
    for step, bit in enumerate(steps[1:]):
        arrived = swap(block, bit, count)
        if step < 2:
            piece, block = fetch(block, block, gate_rows, step * width // 2, width // 2)
            gate.append(piece)
        block = jnp.concatenate([block, arrived])
    send, total, base = encoder(
        (block, swap(block, 0, count)),
        (enc_gain, enc_shift, enc_down_bias, enc_up_bias),
        enc_up,
        enc_down,
        bits,
    )
    arrived = swap(send, 0, count)
    for step, bit in enumerate(range(1, bits)):
        total = total + arrived.astype(jnp.float32)
        arrived = swap(total.astype(jnp.bfloat16), bit, count)
        if step < 2:
            prompts = jnp.concatenate([prompts, swap(prompts, steps[step], count)])
    post = post_norm(total, arrived, base, post_gain, post_shift, prompts)
    features = project(post, swap(post, 0, count), proj_weight, proj_bias, bits)
    for bit in steps[2:]:
        prompts = jnp.concatenate([prompts, swap(prompts, bit, count)])
    for step, bit in enumerate(steps):
        arrived = swap(features, bit, count)
        if step == 0:
            up, features = fetch(features, features, up_rows, 0, width)
        if step == 2:
            down, features = fetch(features, prompts, down_weight, 0, width)
        features = jnp.concatenate([features, arrived])
    features = features, swap(features, 0, count)
    prompts = prompts, swap(prompts, 0, count)
    send, total = language(features, slot_source, prompts, rms_gain, *gate, up, down, bits)
    total = total + swap(send, 0, count).astype(jnp.float32)
    for bit in range(1, bits):
        half = total.shape[0] // 2
        arrived = swap(total[half:].astype(jnp.bfloat16), bit, count)
        total = total[:half] + arrived.astype(jnp.float32)
    return total.astype(jnp.bfloat16)


def any_shards(*arrays):
    count = lax.axis_size("tp")
    bits = count.bit_length() - 1
    whole_tiles = (
        arrays[9].shape[1] % 128 == 0
        and arrays[3].shape[0] % 16 == 0
        and arrays[16].shape[0] % 16 == 0
    )
    if count == 1 << bits and bits > 3 and whole_tiles:
        return fused_shards(bits, *arrays)
    return shards(*arrays)


def solution(mesh):
    placed = (
        P(("groups", "tp"), None),
        P(),
        P(),
        P("tp", None),
        P("tp"),
        P("tp", None),
        P(),
        P(),
        P(),
        P(None, "tp"),
        P("tp"),
        P("groups"),
        P(("groups", "tp"), None),
        P(),
        P(None, "tp"),
        P(None, "tp"),
        P("tp", None),
    )
    return jax.shard_map(
        any_shards, mesh=mesh, in_specs=placed, out_specs=P(("groups", "tp"), None), check_vma=False
    )
```

```python
import functools

import jax
import jax.numpy as jnp
from jax import lax
from jax.experimental import pallas as pl
from jax.experimental.pallas import tpu as pltpu
from jax.sharding import PartitionSpec as P


def mask_of(bit):
    return (1 << bit) | 1 if bit else 1


def slot_of(offset, bits):
    parity = offset & 1
    slot = 0
    for bit in range(1, bits):
        one = (offset >> bit) & 1
        parity = parity ^ one
        slot = slot + (one << (bits - 1 - bit))
    return slot + (parity << (bits - 1))


def offset_of(slot, bits):
    offset = (slot >> (bits - 1)) & 1
    for bit in range(1, bits):
        offset = offset ^ (((slot >> (bits - 1 - bit)) & 1) * mask_of(bit))
    return offset


def swap(value, bit, count):
    pairs = [(i, i ^ mask_of(bit)) for i in range(count)]
    return lax.ppermute(value, "tp", pairs)


def parity_of(index, bits):
    parity = index
    for bit in range(1, bits):
        parity = parity ^ (index >> bit)
    return parity & 1


def in_hbm(value):
    return pltpu.with_memory_space_constraint(value, pltpu.HBM)


def row(ref, part=slice(None)):
    return ref[part].reshape(1, -1)


def dot_last(left, right):
    return lax.dot_general(
        left, right, (((1,), (1,)), ((), ())), preferred_element_type=jnp.float32
    )


def encoder_kernel(
    bits, frames, others, gain, shift, down_bias, bias, up, down, send, keep, base
):
    me = lax.axis_index("tp")
    first = frames.shape[0]
    rows = 2 * first
    pooled = rows // 2
    half = pooled // 2
    own = rows >> bits
    out_row = lax.broadcasted_iota(jnp.int32, (rows, rows), 0)
    in_row = lax.broadcasted_iota(jnp.int32, (rows, rows), 1)
    frame = jnp.where(out_row < pooled, 2 * out_row, 2 * (out_row - pooled) + 1)
    place = slot_of((frame // own) ^ me, bits) * own + frame % own
    order = jnp.where(place == in_row, 1.0, 0.0).astype(jnp.bfloat16)
    values = jnp.dot(
        order, jnp.concatenate([frames[...], others[...]]), preferred_element_type=jnp.float32
    )
    center = values - jnp.mean(values, axis=-1, keepdims=True)
    spread = jnp.mean(center * center, axis=-1, keepdims=True)
    both = (values[:pooled] + values[pooled:]) * 0.5 + row(down_bias)
    normed = (center * lax.rsqrt(spread + 1e-05) * row(gain) + row(shift)).astype(jnp.bfloat16)
    pre_act = dot_last(normed, up[...]) + row(bias).astype(jnp.float32)
    hidden = (0.5 * pre_act * (1.0 + lax.erf(pre_act * 0.7071067811865476))).astype(jnp.bfloat16)
    result = jnp.dot(hidden, down[...], preferred_element_type=jnp.float32)
    mine = (result[:pooled] + result[pooled:]) * 0.5
    upper = parity_of(me, bits) == 1
    keep[...] = jnp.where(upper, mine[half:], mine[:half])
    send[...] = jnp.where(upper, mine[:half], mine[half:]).astype(jnp.bfloat16)
    base[...] = jnp.where(upper, both[half:], both[:half])


def encoder(halves, vectors, up, down, bits):
    first, width = halves[0].shape
    half = first // 2
    vmem = pl.BlockSpec(memory_space=pltpu.VMEM)
    return pl.pallas_call(
        functools.partial(encoder_kernel, bits),
        out_shape=[
            jax.ShapeDtypeStruct((half, width), jnp.bfloat16),
            jax.ShapeDtypeStruct((half, width), jnp.float32),
            jax.ShapeDtypeStruct((half, width), jnp.float32),
        ],
        in_specs=[vmem] * 8,
        out_specs=[vmem] * 3,
        compiler_params=pltpu.CompilerParams(vmem_limit_bytes=8 * 2**20),
        cost_estimate=pl.CostEstimate(
            flops=8 * first * up.size, bytes_accessed=4 * up.size, transcendentals=0
        ),
    )(*halves, *vectors, up, down)


def post_kernel(total, arrived, base, gain, shift, after, post):
    values = total[...] + arrived[...].astype(jnp.float32) + base[...]
    center = values - jnp.mean(values, axis=-1, keepdims=True)
    spread = jnp.mean(center * center, axis=-1, keepdims=True)
    normed = center * lax.rsqrt(spread + 1e-05) * row(gain) + row(shift)
    post[...] = normed.astype(post.dtype)


def post_norm(total, arrived, base, gain, shift, after):
    vmem = pl.BlockSpec(memory_space=pltpu.VMEM)
    return pl.pallas_call(
        post_kernel,
        out_shape=jax.ShapeDtypeStruct(total.shape, jnp.bfloat16),
        in_specs=[vmem] * 5 + [pl.BlockSpec(memory_space=pl.ANY)],
        out_specs=vmem,
        compiler_params=pltpu.CompilerParams(vmem_limit_bytes=4 * 2**20),
    )(total, arrived, base, gain, shift, after)


def project_kernel(bits, post, other, weight, bias, out):
    upper = parity_of(lax.axis_index("tp"), bits) == 1
    low = jnp.where(upper, other[...], post[...])
    high = jnp.where(upper, post[...], other[...])
    every = jnp.concatenate([low, high])
    result = jnp.dot(every, weight[...], preferred_element_type=jnp.float32) + row(bias)
    out[0] = result.astype(out.dtype)


def project(post, other, weight, bias, bits):
    vmem = pl.BlockSpec(memory_space=pltpu.VMEM)
    return pl.pallas_call(
        functools.partial(project_kernel, bits),
        out_shape=jax.ShapeDtypeStruct((1, 2 * post.shape[0], weight.shape[1]), jnp.bfloat16),
        in_specs=[vmem] * 4,
        out_specs=vmem,
        compiler_params=pltpu.CompilerParams(vmem_limit_bytes=4 * 2**20),
    )(post, other, weight, bias)


def stage_kernel(count, *refs):
    sems = refs[2 * count]
    copies = [
        pltpu.make_async_copy(refs[i], refs[count + i], sems.at[i]) for i in range(count)
    ]
    for copy in copies:
        copy.start()
    for copy in copies:
        copy.wait()


def stage(*values):
    count = len(values)
    return pl.pallas_call(
        functools.partial(stage_kernel, count),
        out_shape=[pltpu.VMEM(value.shape, value.dtype) for value in values],
        in_specs=[pl.BlockSpec(memory_space=pltpu.HBM)] * count,
        out_specs=[pl.BlockSpec(memory_space=pltpu.VMEM)] * count,
        scratch_shapes=[pltpu.SemaphoreType.DMA((count,))],
        compiler_params=pltpu.CompilerParams(vmem_limit_bytes=2 * 2**20),
    )(*[in_hbm(value) for value in values])


def fetch_kernel(start, width, carried, after, source, *refs):
    target, passed, sem = refs[-3:]
    part = (slice(None), pl.ds(start, width))
    copy = pltpu.make_async_copy(source.at[part], target.at[part], sem)
    copy.start()
    passed[...] = carried[...]
    copy.wait()


def fetch(carried, after, weight, held, start, width):
    vmem = pl.BlockSpec(memory_space=pltpu.VMEM)
    held = [] if held is None else [held]
    return pl.pallas_call(
        functools.partial(fetch_kernel, start, width),
        out_shape=[
            pltpu.VMEM(weight.shape, weight.dtype),
            jax.ShapeDtypeStruct(carried.shape, carried.dtype),
        ],
        in_specs=[
            vmem,
            pl.BlockSpec(memory_space=pl.ANY),
            pl.BlockSpec(memory_space=pltpu.HBM),
        ]
        + [vmem] * len(held),
        out_specs=[vmem] * 2,
        scratch_shapes=[pltpu.SemaphoreType.DMA],
        input_output_aliases={3: 0} if held else {},
        compiler_params=pltpu.CompilerParams(vmem_limit_bytes=2 * 2**20),
        cost_estimate=pl.CostEstimate(
            flops=0, bytes_accessed=2 * weight.shape[0] * width, transcendentals=0
        ),
    )(carried, after, in_hbm(weight), *held)


def language_kernel(
    bits, near, far, source, prompts, others, gain, gate, up, down,
    send, keep, packed, normed,
):
    count, audio, columns = near.shape
    count = 2 * count
    half, width = prompts.shape
    rows = 2 * half
    own = rows >> bits
    me = lax.axis_index("tp")
    out_row = lax.broadcasted_iota(jnp.int32, (rows, rows), 0)
    in_row = lax.broadcasted_iota(jnp.int32, (rows, rows), 1)
    place = (offset_of(out_row // own, bits) ^ me) * own + out_row % own
    order = jnp.where(place == in_row, 1.0, 0.0).astype(jnp.bfloat16)
    wanted = lax.broadcasted_iota(jnp.int32, (audio, rows), 0)
    chosen = jnp.where(row(source) == wanted, 1.0, 0.0).astype(jnp.bfloat16)
    pick = dot_last(order, chosen)
    audio_row = jnp.sum(pick, axis=1, keepdims=True) > 0.5
    pick = pick.astype(jnp.bfloat16)
    squares = jnp.zeros((rows, columns), jnp.float32)
    for device in range(count):
        part = slice(device * columns, (device + 1) * columns)
        slot = slot_of(me ^ device, bits)
        place = slot & (count // 2 - 1)
        piece = jnp.where(slot < count // 2, near[place], far[place])
        found = jnp.dot(pick, piece, preferred_element_type=jnp.float32)
        prompt = jnp.concatenate([prompts[:, part], others[:, part]])
        value = jnp.where(audio_row, found, prompt.astype(jnp.float32))
        squares += value * value
        packed[:, part] = value.astype(jnp.bfloat16)
    scale = lax.rsqrt(jnp.sum(squares, axis=1, keepdims=True) / width + 1e-06)
    for device in range(count):
        part = slice(device * columns, (device + 1) * columns)
        value = packed[:, part].astype(jnp.float32) * scale * row(gain, part)
        normed[:, part] = value.astype(jnp.bfloat16)
    gated, lifted = dot_last(gate[...], normed[...]), dot_last(up[...], normed[...])
    hidden = (gated * jax.nn.sigmoid(gated) * lifted).T.astype(jnp.bfloat16)
    held = lax.broadcasted_iota(jnp.int32, (half, 1), 0) < own
    pieces = 4
    for piece in range(pieces):
        part = slice(piece * width // pieces, (piece + 1) * width // pieces)
        result = jnp.dot(hidden, down[:, part], preferred_element_type=jnp.float32)
        send[:, part] = result[half:].astype(jnp.bfloat16)
        keep[:, part] = result[:half] + jnp.where(
            held, packed[:half, part].astype(jnp.float32), 0.0
        )


def language(features, source, prompts, gain, gate, up, down, bits):
    half, width = prompts[0].shape
    vmem = pl.BlockSpec(memory_space=pltpu.VMEM)
    return pl.pallas_call(
        functools.partial(language_kernel, bits),
        out_shape=[
            jax.ShapeDtypeStruct((half, width), jnp.bfloat16),
            jax.ShapeDtypeStruct((half, width), jnp.float32),
        ],
        in_specs=[vmem] * 9,
        out_specs=[vmem] * 2,
        scratch_shapes=[pltpu.VMEM((2 * half, width), jnp.bfloat16)] * 2,
        compiler_params=pltpu.CompilerParams(vmem_limit_bytes=12 * 2**20),
        cost_estimate=pl.CostEstimate(
            flops=12 * half * up.size, bytes_accessed=4 * up.size, transcendentals=0
        ),
    )(*features, source, *prompts, gain, gate, up, down)


def layer_norm(values, gain, shift):
    center = values - jnp.mean(values, axis=-1, keepdims=True)
    spread = jnp.mean(center * center, axis=-1, keepdims=True)
    return center * lax.rsqrt(spread + 1e-05) * gain + shift


def to_every(piece, count):
    spread = jnp.broadcast_to(piece[None], (count,) + piece.shape)
    return lax.all_to_all(spread, "tp", 0, 0)


def reduce_rows(partial_value, count):
    rows, width = partial_value.shape
    pieces = partial_value.astype(jnp.bfloat16).reshape(count, rows // count, width)
    return jnp.sum(lax.all_to_all(pieces, "tp", 0, 0).astype(jnp.float32), axis=0)


def pool(values):
    paired = values.reshape(values.shape[0] // 2, 2, values.shape[1])
    return (paired[:, 0, :] + paired[:, 1, :]) * 0.5


def shards(
    frames,
    enc_gain,
    enc_shift,
    enc_up,
    enc_up_bias,
    enc_down,
    enc_down_bias,
    post_gain,
    post_shift,
    proj_weight,
    proj_bias,
    slot_source,
    prompt_embeds,
    rms_gain,
    gate_weight,
    up_weight,
    down_weight,
):
    count = lax.axis_size("tp")
    me = lax.axis_index("tp")
    gathered = to_every(frames, count).reshape(-1, frames.shape[1])
    prompts = to_every(prompt_embeds, count).reshape(-1, prompt_embeds.shape[1])
    normed = layer_norm(gathered.astype(jnp.float32), enc_gain, enc_shift).astype(jnp.bfloat16)
    pre_act = lax.dot_general(
        normed, enc_up, (((1,), (1,)), ((), ())), preferred_element_type=jnp.float32
    )
    hidden = jax.nn.gelu(pre_act + enc_up_bias.astype(jnp.float32), approximate=False)
    partial_value = jnp.dot(
        hidden.astype(jnp.bfloat16), enc_down, preferred_element_type=jnp.float32
    )
    branch = reduce_rows(pool(partial_value), count)
    pooled = pool(frames.astype(jnp.float32)) + branch + enc_down_bias
    post = layer_norm(pooled, post_gain, post_shift).astype(jnp.bfloat16)
    post_every = to_every(post, count).reshape(-1, post.shape[1])
    projected = (
        jnp.dot(post_every, proj_weight, preferred_element_type=jnp.float32) + proj_bias
    ).astype(jnp.bfloat16)
    features = to_every(projected, count)
    features = jnp.transpose(features, (1, 0, 2)).reshape(projected.shape[0], -1)
    clipped = jnp.maximum(slot_source, 0)
    packed = jnp.where(
        (slot_source >= 0)[:, None], jnp.take(features, clipped, axis=0), prompts
    )
    residual = packed.astype(jnp.float32)
    scale = lax.rsqrt(jnp.mean(residual * residual, axis=-1, keepdims=True) + 1e-06)
    lm_normed = (residual * scale * rms_gain).astype(jnp.bfloat16)
    gate = jnp.dot(lm_normed, gate_weight, preferred_element_type=jnp.float32)
    lifted = jnp.dot(lm_normed, up_weight, preferred_element_type=jnp.float32)
    lm_hidden = (jax.nn.silu(gate) * lifted).astype(jnp.bfloat16)
    summed = reduce_rows(
        jnp.dot(lm_hidden, down_weight, preferred_element_type=jnp.float32), count
    )
    row_count = prompt_embeds.shape[0]
    own = lax.dynamic_slice_in_dim(packed, me * row_count, row_count).astype(jnp.float32)
    return (own + summed).astype(jnp.bfloat16)


def fused_shards(
    bits,
    frames,
    enc_gain,
    enc_shift,
    enc_up,
    enc_up_bias,
    enc_down,
    enc_down_bias,
    post_gain,
    post_shift,
    proj_weight,
    proj_bias,
    slot_source,
    prompt_embeds,
    rms_gain,
    gate_weight,
    up_weight,
    down_weight,
):
    count = 1 << bits
    width = prompt_embeds.shape[1]
    steps = range(bits - 1, 0, -1)
    gate_rows, up_rows = gate_weight.T, up_weight.T
    arrived = swap(frames, bits - 1, count)
    prompts_arrived = swap(prompt_embeds, bits - 1, count)
    (
        block, prompts, enc_gain, enc_shift, enc_down_bias, enc_up_bias, enc_up, enc_down,
        post_gain, post_shift, proj_weight, proj_bias, rms_gain, slot_source,
    ) = stage(
        frames, prompt_embeds, enc_gain, enc_shift, enc_down_bias, enc_up_bias, enc_up, enc_down,
        post_gain, post_shift, proj_weight, proj_bias, rms_gain, slot_source,
    )
    gate = up = down = None
    part = width // 4
    large = width // 2 - width // 8
    block = jnp.concatenate([block, arrived])
    prompts = jnp.concatenate([prompts, prompts_arrived])
    for step, bit in enumerate(steps[1:]):
        arrived = swap(block, bit, count)
        if step < 2:
            after = prompts if step else block
            gate, block = fetch(block, after, gate_rows, gate, step * part, part)
        block = jnp.concatenate([block, arrived])
    send, total, base = encoder(
        (block, swap(block, 0, count)),
        (enc_gain, enc_shift, enc_down_bias, enc_up_bias),
        enc_up,
        enc_down,
        bits,
    )
    arrived = swap(send, 0, count)
    for step, bit in enumerate((steps[1], steps[0], *steps[2:])):
        total = total + arrived.astype(jnp.float32)
        outgoing = total.astype(jnp.bfloat16)
        if step != 1:
            outgoing, prompts = lax.optimization_barrier((outgoing, prompts))
        arrived = swap(outgoing, bit, count)
        if step != 1:
            early = prompts
            prompts = jnp.concatenate([prompts, swap(prompts, bit, count)])
        if step == 1:
            gate, total = fetch(total, total, gate_rows, gate, 2 * part, 2 * part)
        elif step < 3:
            up, total = fetch(total, total, up_rows, up, step // 2 * large, large)
    post = post_norm(total, arrived, base, post_gain, post_shift, early)
    features = project(post, swap(post, 0, count), proj_weight, proj_bias, bits)
    for step, bit in enumerate(steps):
        arrived = swap(features, bit, count)
        if step == 1:
            left = width - 2 * large
            up, features = fetch(features, features, up_rows, up, 2 * large, left)
        elif step < 3:
            after = features if step else prompts
            down, features = fetch(features, after, down_weight, down, step * part, 2 * part)
        features = jnp.concatenate([features, arrived])
    features = features, swap(features, 0, count)
    prompts = prompts, swap(prompts, 0, count)
    send, total = language(features, slot_source, prompts, rms_gain, gate, up, down, bits)
    total = total + swap(send, 0, count).astype(jnp.float32)
    for bit in range(1, bits):
        half = total.shape[0] // 2
        arrived = swap(total[half:].astype(jnp.bfloat16), bit, count)
        total = total[:half] + arrived.astype(jnp.float32)
    return total.astype(jnp.bfloat16)


def any_shards(*arrays):
    count = lax.axis_size("tp")
    bits = count.bit_length() - 1
    whole_tiles = (
        arrays[9].shape[1] % 128 == 0
        and arrays[3].shape[0] % 16 == 0
        and arrays[16].shape[0] % 16 == 0
    )
    if count == 1 << bits and bits > 3 and whole_tiles:
        return fused_shards(bits, *arrays)
    return shards(*arrays)


def solution(mesh):
    placed = (
        P(("groups", "tp"), None),
        P(),
        P(),
        P("tp", None),
        P("tp"),
        P("tp", None),
        P(),
        P(),
        P(),
        P(None, "tp"),
        P("tp"),
        P("groups"),
        P(("groups", "tp"), None),
        P(),
        P(None, "tp"),
        P(None, "tp"),
        P("tp", None),
    )
    return jax.shard_map(
        any_shards, mesh=mesh, in_specs=placed, out_specs=P(("groups", "tp"), None), check_vma=False
    )
```

```python
import functools

import jax
import jax.numpy as jnp
from jax import lax
from jax.experimental import pallas as pl
from jax.experimental.pallas import tpu as pltpu
from jax.sharding import PartitionSpec as P


def mask_of(bit):
    return (1 << bit) | 1 if bit else 1


def slot_of(offset, bits):
    parity = offset & 1
    slot = 0
    for bit in range(1, bits):
        one = (offset >> bit) & 1
        parity = parity ^ one
        slot = slot + (one << (bits - 1 - bit))
    return slot + (parity << (bits - 1))


def offset_of(slot, bits):
    offset = (slot >> (bits - 1)) & 1
    for bit in range(1, bits):
        offset = offset ^ (((slot >> (bits - 1 - bit)) & 1) * mask_of(bit))
    return offset


def swap(value, bit, count):
    pairs = [(i, i ^ mask_of(bit)) for i in range(count)]
    return lax.ppermute(value, "tp", pairs)


def parity_of(index, bits):
    parity = index
    for bit in range(1, bits):
        parity = parity ^ (index >> bit)
    return parity & 1


def in_hbm(value):
    return pltpu.with_memory_space_constraint(value, pltpu.HBM)


def row(ref, part=slice(None)):
    return ref[part].reshape(1, -1)


def dot_last(left, right):
    return lax.dot_general(
        left, right, (((1,), (1,)), ((), ())), preferred_element_type=jnp.float32
    )


def group_device(place, parity, bits):
    return 2 * place + (parity ^ parity_of(place, bits))


def encoder_kernel(
    bits, frames, gain, shift, down_bias, bias, bias_pair, up, up_pair, down, down_pair,
    sums, base,
):
    me = lax.axis_index("tp")
    rows = frames.shape[0]
    pooled = rows // 2
    own = rows >> (bits - 1)
    out_row = lax.broadcasted_iota(jnp.int32, (rows, rows), 0)
    in_row = lax.broadcasted_iota(jnp.int32, (rows, rows), 1)
    frame = jnp.where(out_row < pooled, 2 * out_row, 2 * (out_row - pooled) + 1)
    device = group_device(frame // own, parity_of(me, bits), bits)
    place = slot_of(device ^ me, bits) * own + frame % own
    order = jnp.where(place == in_row, 1.0, 0.0).astype(jnp.bfloat16)
    values = jnp.dot(order, frames[...], preferred_element_type=jnp.float32)
    center = values - jnp.mean(values, axis=-1, keepdims=True)
    spread = jnp.mean(center * center, axis=-1, keepdims=True)
    base[...] = (values[:pooled] + values[pooled:]) * 0.5 + row(down_bias)
    normed = (center * lax.rsqrt(spread + 1e-05) * row(gain) + row(shift)).astype(jnp.bfloat16)
    result = 0.0
    for weight, offset, back in ((up, bias, down), (up_pair, bias_pair, down_pair)):
        pre_act = dot_last(normed, weight[...]) + row(offset).astype(jnp.float32)
        hidden = 0.5 * pre_act * (1.0 + lax.erf(pre_act * 0.7071067811865476))
        result += jnp.dot(
            hidden.astype(jnp.bfloat16), back[...], preferred_element_type=jnp.float32
        )
    sums[...] = (result[:pooled] + result[pooled:]) * 0.5


def encoder(frames, vectors, ups, downs, bits):
    rows, width = frames.shape
    vmem = pl.BlockSpec(memory_space=pltpu.VMEM)
    return pl.pallas_call(
        functools.partial(encoder_kernel, bits),
        out_shape=[jax.ShapeDtypeStruct((rows // 2, width), jnp.float32)] * 2,
        in_specs=[vmem] * 10,
        out_specs=[vmem] * 2,
        compiler_params=pltpu.CompilerParams(vmem_limit_bytes=8 * 2**20),
        cost_estimate=pl.CostEstimate(
            flops=8 * rows * ups[0].size, bytes_accessed=8 * ups[0].size, transcendentals=0
        ),
    )(frames, *vectors, *ups, *downs)


def post_kernel(total, arrived, base, gain, shift, after, post):
    values = total[...] + arrived[...].astype(jnp.float32) + base[...]
    center = values - jnp.mean(values, axis=-1, keepdims=True)
    spread = jnp.mean(center * center, axis=-1, keepdims=True)
    normed = center * lax.rsqrt(spread + 1e-05) * row(gain) + row(shift)
    post[...] = normed.astype(post.dtype)


def post_norm(total, arrived, base, gain, shift, after):
    vmem = pl.BlockSpec(memory_space=pltpu.VMEM)
    return pl.pallas_call(
        post_kernel,
        out_shape=jax.ShapeDtypeStruct(total.shape, jnp.bfloat16),
        in_specs=[vmem] * 5 + [pl.BlockSpec(memory_space=pl.ANY)],
        out_specs=vmem,
        compiler_params=pltpu.CompilerParams(vmem_limit_bytes=4 * 2**20),
    )(total, arrived, base, gain, shift, after)


def project_kernel(post, weight, weight_pair, bias, bias_pair, out):
    for i, (shard, offset) in enumerate(((weight, bias), (weight_pair, bias_pair))):
        result = jnp.dot(post[...], shard[...], preferred_element_type=jnp.float32)
        out[0, i] = (result + row(offset)).astype(out.dtype)


def project(post, weights, biases):
    vmem = pl.BlockSpec(memory_space=pltpu.VMEM)
    return pl.pallas_call(
        project_kernel,
        out_shape=jax.ShapeDtypeStruct(
            (1, 2, post.shape[0], weights[0].shape[1]), jnp.bfloat16
        ),
        in_specs=[vmem] * 5,
        out_specs=vmem,
        compiler_params=pltpu.CompilerParams(vmem_limit_bytes=4 * 2**20),
    )(post, *weights, *biases)


def stage_kernel(count, *refs):
    sems = refs[2 * count]
    copies = [
        pltpu.make_async_copy(refs[i], refs[count + i], sems.at[i]) for i in range(count)
    ]
    for copy in copies:
        copy.start()
    for copy in copies:
        copy.wait()


def stage(*values):
    count = len(values)
    return pl.pallas_call(
        functools.partial(stage_kernel, count),
        out_shape=[pltpu.VMEM(value.shape, value.dtype) for value in values],
        in_specs=[pl.BlockSpec(memory_space=pltpu.HBM)] * count,
        out_specs=[pl.BlockSpec(memory_space=pltpu.VMEM)] * count,
        scratch_shapes=[pltpu.SemaphoreType.DMA((count,))],
        compiler_params=pltpu.CompilerParams(vmem_limit_bytes=2 * 2**20),
    )(*[in_hbm(value) for value in values])


def fetch_kernel(start, width, carried, after, source, *refs):
    target, passed, sem = refs[-3:]
    part = (slice(None), pl.ds(start, width))
    copy = pltpu.make_async_copy(source.at[part], target.at[part], sem)
    copy.start()
    passed[...] = carried[...]
    copy.wait()


def fetch(carried, after, weight, held, start, width):
    vmem = pl.BlockSpec(memory_space=pltpu.VMEM)
    held = [] if held is None else [held]
    return pl.pallas_call(
        functools.partial(fetch_kernel, start, width),
        out_shape=[
            pltpu.VMEM(weight.shape, weight.dtype),
            jax.ShapeDtypeStruct(carried.shape, carried.dtype),
        ],
        in_specs=[
            vmem,
            pl.BlockSpec(memory_space=pl.ANY),
            pl.BlockSpec(memory_space=pltpu.HBM),
        ]
        + [vmem] * len(held),
        out_specs=[vmem] * 2,
        scratch_shapes=[pltpu.SemaphoreType.DMA],
        input_output_aliases={3: 0} if held else {},
        compiler_params=pltpu.CompilerParams(vmem_limit_bytes=2 * 2**20),
        cost_estimate=pl.CostEstimate(
            flops=0, bytes_accessed=2 * weight.shape[0] * width, transcendentals=0
        ),
    )(carried, after, in_hbm(weight), *held)


def language_kernel(
    bits, near, far, source, prompts, others, gain, gate, up, down,
    send, keep, packed, normed,
):
    count, group, columns = 1 << bits, near.shape[2], near.shape[3]
    half, width = prompts.shape
    rows = 2 * half
    own = rows >> bits
    me = lax.axis_index("tp")
    out_row = lax.broadcasted_iota(jnp.int32, (rows, rows), 0)
    in_row = lax.broadcasted_iota(jnp.int32, (rows, rows), 1)
    place = (offset_of(out_row // own, bits) ^ me) * own + out_row % own
    order = jnp.where(place == in_row, 1.0, 0.0).astype(jnp.bfloat16)
    parity = parity_of(me, bits)
    audio = lax.broadcasted_iota(jnp.int32, (2 * group, rows), 0)
    parities = jnp.where(audio < group, parity, 1 - parity)
    audio = jnp.where(audio < group, audio, audio - group)
    each = group >> (bits - 1)
    wanted = group_device(audio // each, parities, bits) * each + audio % each
    chosen = jnp.where(row(source) == wanted, 1.0, 0.0).astype(jnp.bfloat16)
    pick = dot_last(order, chosen)
    audio_row = jnp.sum(pick, axis=1, keepdims=True) > 0.5
    pick = pick.astype(jnp.bfloat16)
    squares = jnp.zeros((rows, columns), jnp.float32)
    for device in range(count):
        part = slice(device * columns, (device + 1) * columns)
        differs = parity ^ parity_of(device, bits)
        near_slot = slot_of(me ^ device ^ differs, bits)
        far_slot = slot_of(me ^ device ^ differs, bits)
        piece = jnp.concatenate([near[near_slot, differs], far[far_slot, 1 - differs]])
        found = jnp.dot(pick, piece, preferred_element_type=jnp.float32)
        prompt = jnp.concatenate([prompts[:, part], others[:, part]])
        value = jnp.where(audio_row, found, prompt.astype(jnp.float32))
        squares += value * value
        packed[:, part] = value.astype(jnp.bfloat16)
    scale = lax.rsqrt(jnp.sum(squares, axis=1, keepdims=True) / width + 1e-06)
    for device in range(count):
        part = slice(device * columns, (device + 1) * columns)
        value = packed[:, part].astype(jnp.float32) * scale * row(gain, part)
        normed[:, part] = value.astype(jnp.bfloat16)
    gated, lifted = dot_last(gate[...], normed[...]), dot_last(up[...], normed[...])
    hidden = (gated * jax.nn.sigmoid(gated) * lifted).T.astype(jnp.bfloat16)
    held = lax.broadcasted_iota(jnp.int32, (half, 1), 0) < own
    pieces = 4
    for piece in range(pieces):
        part = slice(piece * width // pieces, (piece + 1) * width // pieces)
        result = jnp.dot(hidden, down[:, part], preferred_element_type=jnp.float32)
        send[:, part] = result[half:].astype(jnp.bfloat16)
        keep[:, part] = result[:half] + jnp.where(
            held, packed[:half, part].astype(jnp.float32), 0.0
        )


def language(features, source, prompts, gain, gate, up, down, bits):
    half, width = prompts[0].shape
    vmem = pl.BlockSpec(memory_space=pltpu.VMEM)
    return pl.pallas_call(
        functools.partial(language_kernel, bits),
        out_shape=[
            jax.ShapeDtypeStruct((half, width), jnp.bfloat16),
            jax.ShapeDtypeStruct((half, width), jnp.float32),
        ],
        in_specs=[vmem] * 9,
        out_specs=[vmem] * 2,
        scratch_shapes=[pltpu.VMEM((2 * half, width), jnp.bfloat16)] * 2,
        compiler_params=pltpu.CompilerParams(vmem_limit_bytes=12 * 2**20),
        cost_estimate=pl.CostEstimate(
            flops=12 * half * up.size, bytes_accessed=4 * up.size, transcendentals=0
        ),
    )(*features, source, *prompts, gain, gate, up, down)


def layer_norm(values, gain, shift):
    center = values - jnp.mean(values, axis=-1, keepdims=True)
    spread = jnp.mean(center * center, axis=-1, keepdims=True)
    return center * lax.rsqrt(spread + 1e-05) * gain + shift


def to_every(piece, count):
    spread = jnp.broadcast_to(piece[None], (count,) + piece.shape)
    return lax.all_to_all(spread, "tp", 0, 0)


def reduce_rows(partial_value, count):
    rows, width = partial_value.shape
    pieces = partial_value.astype(jnp.bfloat16).reshape(count, rows // count, width)
    return jnp.sum(lax.all_to_all(pieces, "tp", 0, 0).astype(jnp.float32), axis=0)


def pool(values):
    paired = values.reshape(values.shape[0] // 2, 2, values.shape[1])
    return (paired[:, 0, :] + paired[:, 1, :]) * 0.5


def shards(
    frames,
    enc_gain,
    enc_shift,
    enc_up,
    enc_up_bias,
    enc_down,
    enc_down_bias,
    post_gain,
    post_shift,
    proj_weight,
    proj_bias,
    slot_source,
    prompt_embeds,
    rms_gain,
    gate_weight,
    up_weight,
    down_weight,
):
    count = lax.axis_size("tp")
    me = lax.axis_index("tp")
    gathered = to_every(frames, count).reshape(-1, frames.shape[1])
    prompts = to_every(prompt_embeds, count).reshape(-1, prompt_embeds.shape[1])
    normed = layer_norm(gathered.astype(jnp.float32), enc_gain, enc_shift).astype(jnp.bfloat16)
    pre_act = lax.dot_general(
        normed, enc_up, (((1,), (1,)), ((), ())), preferred_element_type=jnp.float32
    )
    hidden = jax.nn.gelu(pre_act + enc_up_bias.astype(jnp.float32), approximate=False)
    partial_value = jnp.dot(
        hidden.astype(jnp.bfloat16), enc_down, preferred_element_type=jnp.float32
    )
    branch = reduce_rows(pool(partial_value), count)
    pooled = pool(frames.astype(jnp.float32)) + branch + enc_down_bias
    post = layer_norm(pooled, post_gain, post_shift).astype(jnp.bfloat16)
    post_every = to_every(post, count).reshape(-1, post.shape[1])
    projected = (
        jnp.dot(post_every, proj_weight, preferred_element_type=jnp.float32) + proj_bias
    ).astype(jnp.bfloat16)
    features = to_every(projected, count)
    features = jnp.transpose(features, (1, 0, 2)).reshape(projected.shape[0], -1)
    clipped = jnp.maximum(slot_source, 0)
    packed = jnp.where(
        (slot_source >= 0)[:, None], jnp.take(features, clipped, axis=0), prompts
    )
    residual = packed.astype(jnp.float32)
    scale = lax.rsqrt(jnp.mean(residual * residual, axis=-1, keepdims=True) + 1e-06)
    lm_normed = (residual * scale * rms_gain).astype(jnp.bfloat16)
    gate = jnp.dot(lm_normed, gate_weight, preferred_element_type=jnp.float32)
    lifted = jnp.dot(lm_normed, up_weight, preferred_element_type=jnp.float32)
    lm_hidden = (jax.nn.silu(gate) * lifted).astype(jnp.bfloat16)
    summed = reduce_rows(
        jnp.dot(lm_hidden, down_weight, preferred_element_type=jnp.float32), count
    )
    row_count = prompt_embeds.shape[0]
    own = lax.dynamic_slice_in_dim(packed, me * row_count, row_count).astype(jnp.float32)
    return (own + summed).astype(jnp.bfloat16)


def fused_shards(
    bits,
    frames,
    enc_gain,
    enc_shift,
    enc_up,
    enc_up_bias,
    enc_down,
    enc_down_bias,
    post_gain,
    post_shift,
    proj_weight,
    proj_bias,
    slot_source,
    prompt_embeds,
    rms_gain,
    gate_weight,
    up_weight,
    down_weight,
):
    count = 1 << bits
    width = prompt_embeds.shape[1]
    steps = range(bits - 1, 0, -1)
    gate_rows, up_rows = gate_weight.T, up_weight.T
    arrived = swap(frames, bits - 1, count)
    prompts_arrived = swap(prompt_embeds, bits - 1, count)
    up_pair, down_pair, bias_pair, proj_pair, proj_bias_pair = [
        swap(value, 0, count)
        for value in (enc_up, enc_down, enc_up_bias, proj_weight, proj_bias)
    ]
    (
        block, prompts, enc_gain, enc_shift, enc_down_bias, enc_up_bias, enc_up, enc_down,
        post_gain, post_shift, proj_weight, proj_bias, rms_gain, slot_source,
    ) = stage(
        frames, prompt_embeds, enc_gain, enc_shift, enc_down_bias, enc_up_bias, enc_up, enc_down,
        post_gain, post_shift, proj_weight, proj_bias, rms_gain, slot_source,
    )
    gate = up = down = None
    part = width // 4
    large = width // 2 - width // 8
    block = jnp.concatenate([block, arrived])
    prompts = jnp.concatenate([prompts, prompts_arrived])
    for step, bit in enumerate(steps[1:]):
        arrived = swap(block, bit, count)
        if step < 2:
            after = prompts if step else block
            gate, block = fetch(block, after, gate_rows, gate, step * part, part)
        block = jnp.concatenate([block, arrived])
    total, base = encoder(
        block,
        (enc_gain, enc_shift, enc_down_bias, enc_up_bias, bias_pair),
        (enc_up, up_pair),
        (enc_down, down_pair),
        bits,
    )
    arrived = None
    for step, bit in enumerate((steps[1], steps[0], *steps[2:])):
        if arrived is not None:
            total = total + arrived.astype(jnp.float32)
        outgoing = total.astype(jnp.bfloat16)
        if step != 1:
            outgoing, prompts = lax.optimization_barrier((outgoing, prompts))
        arrived = swap(outgoing, bit, count)
        if step != 1:
            early = prompts
            prompts = jnp.concatenate([prompts, swap(prompts, bit, count)])
        if step == 1:
            gate, total = fetch(total, total, gate_rows, gate, 2 * part, 2 * part)
        elif step < 3:
            up, total = fetch(total, total, up_rows, up, step // 2 * large, large)
    post = post_norm(total, arrived, base, post_gain, post_shift, early)
    features = project(post, (proj_weight, proj_pair), (proj_bias, proj_bias_pair))
    for step, bit in enumerate(steps):
        arrived = swap(features, bit, count)
        if step == 1:
            left = width - 2 * large
            up, features = fetch(features, features, up_rows, up, 2 * large, left)
        elif step < 3:
            after = prompts if step else features
            down, features = fetch(features, after, down_weight, down, step * part, 2 * part)
        features = jnp.concatenate([features, arrived])
    features = features, swap(features, 0, count)
    prompts = prompts, swap(prompts, 0, count)
    send, total = language(features, slot_source, prompts, rms_gain, gate, up, down, bits)
    total = total + swap(send, 0, count).astype(jnp.float32)
    for bit in range(1, bits):
        half = total.shape[0] // 2
        arrived = swap(total[half:].astype(jnp.bfloat16), bit, count)
        total = total[:half] + arrived.astype(jnp.float32)
    return total.astype(jnp.bfloat16)


def any_shards(*arrays):
    count = lax.axis_size("tp")
    bits = count.bit_length() - 1
    whole_tiles = (
        arrays[9].shape[1] % 128 == 0
        and arrays[3].shape[0] % 16 == 0
        and arrays[16].shape[0] % 16 == 0
    )
    if count == 1 << bits and bits > 3 and whole_tiles:
        return fused_shards(bits, *arrays)
    return shards(*arrays)


def solution(mesh):
    placed = (
        P(("groups", "tp"), None),
        P(),
        P(),
        P("tp", None),
        P("tp"),
        P("tp", None),
        P(),
        P(),
        P(),
        P(None, "tp"),
        P("tp"),
        P("groups"),
        P(("groups", "tp"), None),
        P(),
        P(None, "tp"),
        P(None, "tp"),
        P("tp", None),
    )
    return jax.shard_map(
        any_shards, mesh=mesh, in_specs=placed, out_specs=P(("groups", "tp"), None), check_vma=False
    )
```

```python
import functools

import jax
import jax.numpy as jnp
from jax import lax
from jax.experimental import pallas as pl
from jax.experimental.pallas import tpu as pltpu
from jax.sharding import PartitionSpec as P


def mask_of(bit):
    return (1 << bit) | 1 if bit else 1


def slot_of(offset, bits):
    parity = offset & 1
    slot = 0
    for bit in range(1, bits):
        one = (offset >> bit) & 1
        parity = parity ^ one
        slot = slot + (one << (bits - 1 - bit))
    return slot + (parity << (bits - 1))


def offset_of(slot, bits):
    offset = (slot >> (bits - 1)) & 1
    for bit in range(1, bits):
        offset = offset ^ (((slot >> (bits - 1 - bit)) & 1) * mask_of(bit))
    return offset


def swap(value, bit, count):
    pairs = [(i, i ^ mask_of(bit)) for i in range(count)]
    return lax.ppermute(value, "tp", pairs)


def parity_of(index, bits):
    parity = index
    for bit in range(1, bits):
        parity = parity ^ (index >> bit)
    return parity & 1


def in_hbm(value):
    return pltpu.with_memory_space_constraint(value, pltpu.HBM)


def row(ref, part=slice(None)):
    return ref[part].reshape(1, -1)


def dot_last(left, right):
    return lax.dot_general(
        left, right, (((1,), (1,)), ((), ())), preferred_element_type=jnp.float32
    )


def group_device(place, parity, bits):
    return 2 * place + (parity ^ parity_of(place, bits))


def encoder_kernel(
    bits, frames, gain, shift, down_bias, bias, bias_pair, up, up_pair, down, down_pair,
    sums, base,
):
    me = lax.axis_index("tp")
    rows = frames.shape[0]
    pooled = rows // 2
    own = rows >> (bits - 1)
    out_row = lax.broadcasted_iota(jnp.int32, (rows, rows), 0)
    in_row = lax.broadcasted_iota(jnp.int32, (rows, rows), 1)
    frame = jnp.where(out_row < pooled, 2 * out_row, 2 * (out_row - pooled) + 1)
    device = group_device(frame // own, parity_of(me, bits), bits)
    place = slot_of(device ^ me, bits) * own + frame % own
    order = jnp.where(place == in_row, 1.0, 0.0).astype(jnp.bfloat16)
    values = jnp.dot(order, frames[...], preferred_element_type=jnp.float32)
    center = values - jnp.mean(values, axis=-1, keepdims=True)
    spread = jnp.mean(center * center, axis=-1, keepdims=True)
    base[...] = (values[:pooled] + values[pooled:]) * 0.5 + row(down_bias)
    normed = (center * lax.rsqrt(spread + 1e-05) * row(gain) + row(shift)).astype(jnp.bfloat16)
    result = 0.0
    for weight, offset, back in ((up, bias, down), (up_pair, bias_pair, down_pair)):
        pre_act = dot_last(normed, weight[...]) + row(offset).astype(jnp.float32)
        hidden = 0.5 * pre_act * (1.0 + lax.erf(pre_act * 0.7071067811865476))
        result += jnp.dot(
            hidden.astype(jnp.bfloat16), back[...], preferred_element_type=jnp.float32
        )
    sums[...] = (result[:pooled] + result[pooled:]) * 0.5


def encoder(frames, vectors, ups, downs, bits):
    rows, width = frames.shape
    vmem = pl.BlockSpec(memory_space=pltpu.VMEM)
    return pl.pallas_call(
        functools.partial(encoder_kernel, bits),
        out_shape=[jax.ShapeDtypeStruct((rows // 2, width), jnp.float32)] * 2,
        in_specs=[vmem] * 10,
        out_specs=[vmem] * 2,
        compiler_params=pltpu.CompilerParams(vmem_limit_bytes=8 * 2**20),
        cost_estimate=pl.CostEstimate(
            flops=8 * rows * ups[0].size, bytes_accessed=8 * ups[0].size, transcendentals=0
        ),
    )(frames, *vectors, *ups, *downs)


def post_kernel(total, arrived, base, gain, shift, after, post):
    values = total[...] + arrived[...].astype(jnp.float32) + base[...]
    center = values - jnp.mean(values, axis=-1, keepdims=True)
    spread = jnp.mean(center * center, axis=-1, keepdims=True)
    normed = center * lax.rsqrt(spread + 1e-05) * row(gain) + row(shift)
    post[...] = normed.astype(post.dtype)


def post_norm(total, arrived, base, gain, shift, after):
    vmem = pl.BlockSpec(memory_space=pltpu.VMEM)
    return pl.pallas_call(
        post_kernel,
        out_shape=jax.ShapeDtypeStruct(total.shape, jnp.bfloat16),
        in_specs=[vmem] * 5 + [pl.BlockSpec(memory_space=pl.ANY)],
        out_specs=vmem,
        compiler_params=pltpu.CompilerParams(vmem_limit_bytes=4 * 2**20),
    )(total, arrived, base, gain, shift, after)


def project_kernel(post, weight, weight_pair, bias, bias_pair, out):
    for i, (shard, offset) in enumerate(((weight, bias), (weight_pair, bias_pair))):
        result = jnp.dot(post[...], shard[...], preferred_element_type=jnp.float32)
        out[0, i] = (result + row(offset)).astype(out.dtype)


def project(post, weights, biases):
    vmem = pl.BlockSpec(memory_space=pltpu.VMEM)
    return pl.pallas_call(
        project_kernel,
        out_shape=jax.ShapeDtypeStruct(
            (1, 2, post.shape[0], weights[0].shape[1]), jnp.bfloat16
        ),
        in_specs=[vmem] * 5,
        out_specs=vmem,
        compiler_params=pltpu.CompilerParams(vmem_limit_bytes=4 * 2**20),
    )(post, *weights, *biases)


def stage_kernel(count, extra, carry, *refs):
    sources, sems = refs[:count], refs[-1]
    targets = refs[count + extra + carry :][:count]
    copies = [
        pltpu.make_async_copy(source, target, sems.at[i])
        for i, (source, target) in enumerate(zip(sources, targets))
    ]
    for copy in copies:
        copy.start()
    if carry:
        refs[-2][...] = refs[count][...]
    for copy in copies:
        copy.wait()


def stage(values, *carried, after=()):
    count, carry = len(values), len(carried)
    vmem = pl.BlockSpec(memory_space=pltpu.VMEM)
    return pl.pallas_call(
        functools.partial(stage_kernel, count, len(after), carry),
        out_shape=[pltpu.VMEM(value.shape, value.dtype) for value in values]
        + [jax.ShapeDtypeStruct(value.shape, value.dtype) for value in carried],
        in_specs=[pl.BlockSpec(memory_space=pltpu.HBM)] * count
        + [vmem] * carry
        + [pl.BlockSpec(memory_space=pl.ANY)] * len(after),
        out_specs=[vmem] * (count + carry),
        scratch_shapes=[pltpu.SemaphoreType.DMA((count,))],
        compiler_params=pltpu.CompilerParams(vmem_limit_bytes=2 * 2**20),
        cost_estimate=pl.CostEstimate(
            flops=0, bytes_accessed=2 * sum(value.size for value in values), transcendentals=0
        ),
    )(*[in_hbm(value) for value in values], *carried, *after)


def fetch_kernel(start, width, carried, after, source, *refs):
    target, passed, sem = refs[-3:]
    part = (slice(None), pl.ds(start, width))
    copy = pltpu.make_async_copy(source.at[part], target.at[part], sem)
    copy.start()
    passed[...] = carried[...]
    copy.wait()


def fetch(carried, after, weight, held, start, width):
    vmem = pl.BlockSpec(memory_space=pltpu.VMEM)
    held = [] if held is None else [held]
    return pl.pallas_call(
        functools.partial(fetch_kernel, start, width),
        out_shape=[
            pltpu.VMEM(weight.shape, weight.dtype),
            jax.ShapeDtypeStruct(carried.shape, carried.dtype),
        ],
        in_specs=[
            vmem,
            pl.BlockSpec(memory_space=pl.ANY),
            pl.BlockSpec(memory_space=pltpu.HBM),
        ]
        + [vmem] * len(held),
        out_specs=[vmem] * 2,
        scratch_shapes=[pltpu.SemaphoreType.DMA],
        input_output_aliases={3: 0} if held else {},
        compiler_params=pltpu.CompilerParams(vmem_limit_bytes=2 * 2**20),
        cost_estimate=pl.CostEstimate(
            flops=0, bytes_accessed=2 * weight.shape[0] * width, transcendentals=0
        ),
    )(carried, after, in_hbm(weight), *held)


def language_kernel(
    bits, near, far, source, prompts, others, gain, gate, up, down, down_hbm,
    send, keep, packed, normed, rest, sem,
):
    count, group, columns = 1 << bits, near.shape[2], near.shape[3]
    half, width = prompts.shape
    cut = width // 2
    copy = pltpu.make_async_copy(down_hbm.at[:, pl.ds(cut, cut)], rest, sem)
    copy.start()
    rows = 2 * half
    own = rows >> bits
    me = lax.axis_index("tp")
    out_row = lax.broadcasted_iota(jnp.int32, (rows, rows), 0)
    in_row = lax.broadcasted_iota(jnp.int32, (rows, rows), 1)
    place = (offset_of(out_row // own, bits) ^ me) * own + out_row % own
    order = jnp.where(place == in_row, 1.0, 0.0).astype(jnp.bfloat16)
    parity = parity_of(me, bits)
    audio = lax.broadcasted_iota(jnp.int32, (2 * group, rows), 0)
    parities = jnp.where(audio < group, parity, 1 - parity)
    audio = jnp.where(audio < group, audio, audio - group)
    each = group >> (bits - 1)
    wanted = group_device(audio // each, parities, bits) * each + audio % each
    chosen = jnp.where(row(source) == wanted, 1.0, 0.0).astype(jnp.bfloat16)
    pick = dot_last(order, chosen)
    audio_row = jnp.sum(pick, axis=1, keepdims=True) > 0.5
    pick = pick.astype(jnp.bfloat16)
    squares = jnp.zeros((rows, columns), jnp.float32)
    for device in range(count):
        part = slice(device * columns, (device + 1) * columns)
        differs = parity ^ parity_of(device, bits)
        near_slot = slot_of(me ^ device ^ differs, bits)
        far_slot = slot_of(me ^ device ^ differs, bits)
        piece = jnp.concatenate([near[near_slot, differs], far[far_slot, 1 - differs]])
        found = jnp.dot(pick, piece, preferred_element_type=jnp.float32)
        prompt = jnp.concatenate([prompts[:, part], others[:, part]])
        value = jnp.where(audio_row, found, prompt.astype(jnp.float32))
        squares += value * value
        packed[:, part] = value.astype(jnp.bfloat16)
    scale = lax.rsqrt(jnp.sum(squares, axis=1, keepdims=True) / width + 1e-06)
    for device in range(count):
        part = slice(device * columns, (device + 1) * columns)
        value = packed[:, part].astype(jnp.float32) * scale * row(gain, part)
        normed[:, part] = value.astype(jnp.bfloat16)
    gated, lifted = dot_last(gate[...], normed[...]), dot_last(up[...], normed[...])
    hidden = (gated * jax.nn.sigmoid(gated) * lifted).T.astype(jnp.bfloat16)
    held = lax.broadcasted_iota(jnp.int32, (half, 1), 0) < own
    pieces = 4
    for piece in range(pieces):
        part = slice(piece * width // pieces, (piece + 1) * width // pieces)
        if part.start == cut:
            copy.wait()
        if part.start < cut:
            weight = down[:, part]
        else:
            weight = rest[:, part.start - cut : part.stop - cut]
        result = jnp.dot(hidden, weight, preferred_element_type=jnp.float32)
        send[:, part] = result[half:].astype(jnp.bfloat16)
        keep[:, part] = result[:half] + jnp.where(
            held, packed[:half, part].astype(jnp.float32), 0.0
        )


def language(features, source, prompts, gain, gate, up, down, down_weight, bits):
    half, width = prompts[0].shape
    vmem = pl.BlockSpec(memory_space=pltpu.VMEM)
    return pl.pallas_call(
        functools.partial(language_kernel, bits),
        out_shape=[
            jax.ShapeDtypeStruct((half, width), jnp.bfloat16),
            jax.ShapeDtypeStruct((half, width), jnp.float32),
        ],
        in_specs=[vmem] * 9 + [pl.BlockSpec(memory_space=pltpu.HBM)],
        out_specs=[vmem] * 2,
        scratch_shapes=[pltpu.VMEM((2 * half, width), jnp.bfloat16)] * 2
        + [pltpu.VMEM((down.shape[0], width // 2), down.dtype), pltpu.SemaphoreType.DMA],
        compiler_params=pltpu.CompilerParams(vmem_limit_bytes=12 * 2**20),
        cost_estimate=pl.CostEstimate(
            flops=12 * half * up.size, bytes_accessed=4 * up.size, transcendentals=0
        ),
    )(*features, source, *prompts, gain, gate, up, down, in_hbm(down_weight))


def layer_norm(values, gain, shift):
    center = values - jnp.mean(values, axis=-1, keepdims=True)
    spread = jnp.mean(center * center, axis=-1, keepdims=True)
    return center * lax.rsqrt(spread + 1e-05) * gain + shift


def to_every(piece, count):
    spread = jnp.broadcast_to(piece[None], (count,) + piece.shape)
    return lax.all_to_all(spread, "tp", 0, 0)


def reduce_rows(partial_value, count):
    rows, width = partial_value.shape
    pieces = partial_value.astype(jnp.bfloat16).reshape(count, rows // count, width)
    return jnp.sum(lax.all_to_all(pieces, "tp", 0, 0).astype(jnp.float32), axis=0)


def pool(values):
    paired = values.reshape(values.shape[0] // 2, 2, values.shape[1])
    return (paired[:, 0, :] + paired[:, 1, :]) * 0.5


def shards(
    frames,
    enc_gain,
    enc_shift,
    enc_up,
    enc_up_bias,
    enc_down,
    enc_down_bias,
    post_gain,
    post_shift,
    proj_weight,
    proj_bias,
    slot_source,
    prompt_embeds,
    rms_gain,
    gate_weight,
    up_weight,
    down_weight,
):
    count = lax.axis_size("tp")
    me = lax.axis_index("tp")
    gathered = to_every(frames, count).reshape(-1, frames.shape[1])
    prompts = to_every(prompt_embeds, count).reshape(-1, prompt_embeds.shape[1])
    normed = layer_norm(gathered.astype(jnp.float32), enc_gain, enc_shift).astype(jnp.bfloat16)
    pre_act = lax.dot_general(
        normed, enc_up, (((1,), (1,)), ((), ())), preferred_element_type=jnp.float32
    )
    hidden = jax.nn.gelu(pre_act + enc_up_bias.astype(jnp.float32), approximate=False)
    partial_value = jnp.dot(
        hidden.astype(jnp.bfloat16), enc_down, preferred_element_type=jnp.float32
    )
    branch = reduce_rows(pool(partial_value), count)
    pooled = pool(frames.astype(jnp.float32)) + branch + enc_down_bias
    post = layer_norm(pooled, post_gain, post_shift).astype(jnp.bfloat16)
    post_every = to_every(post, count).reshape(-1, post.shape[1])
    projected = (
        jnp.dot(post_every, proj_weight, preferred_element_type=jnp.float32) + proj_bias
    ).astype(jnp.bfloat16)
    features = to_every(projected, count)
    features = jnp.transpose(features, (1, 0, 2)).reshape(projected.shape[0], -1)
    clipped = jnp.maximum(slot_source, 0)
    packed = jnp.where(
        (slot_source >= 0)[:, None], jnp.take(features, clipped, axis=0), prompts
    )
    residual = packed.astype(jnp.float32)
    scale = lax.rsqrt(jnp.mean(residual * residual, axis=-1, keepdims=True) + 1e-06)
    lm_normed = (residual * scale * rms_gain).astype(jnp.bfloat16)
    gate = jnp.dot(lm_normed, gate_weight, preferred_element_type=jnp.float32)
    lifted = jnp.dot(lm_normed, up_weight, preferred_element_type=jnp.float32)
    lm_hidden = (jax.nn.silu(gate) * lifted).astype(jnp.bfloat16)
    summed = reduce_rows(
        jnp.dot(lm_hidden, down_weight, preferred_element_type=jnp.float32), count
    )
    row_count = prompt_embeds.shape[0]
    own = lax.dynamic_slice_in_dim(packed, me * row_count, row_count).astype(jnp.float32)
    return (own + summed).astype(jnp.bfloat16)


def fused_shards(
    bits,
    frames,
    enc_gain,
    enc_shift,
    enc_up,
    enc_up_bias,
    enc_down,
    enc_down_bias,
    post_gain,
    post_shift,
    proj_weight,
    proj_bias,
    slot_source,
    prompt_embeds,
    rms_gain,
    gate_weight,
    up_weight,
    down_weight,
):
    count = 1 << bits
    width = prompt_embeds.shape[1]
    steps = range(bits - 1, 0, -1)
    gate_rows, up_rows = gate_weight.T, up_weight.T
    arrived = swap(frames, bits - 1, count)
    prompts_arrived = swap(prompt_embeds, bits - 1, count)
    up_pair, down_pair, bias_pair, proj_pair, proj_bias_pair = [
        swap(value, 0, count)
        for value in (enc_up, enc_down, enc_up_bias, proj_weight, proj_bias)
    ]
    block, prompts, enc_gain, enc_shift = stage((frames, prompt_embeds, enc_gain, enc_shift))
    gate = up = down = None
    part = width // 4
    large = width // 2 - width // 8
    block = jnp.concatenate([block, arrived])
    prompts = jnp.concatenate([prompts, prompts_arrived])
    for step, bit in enumerate(steps[1:]):
        arrived = swap(block, bit, count)
        if step == 0:
            gate, block = fetch(block, block, gate_rows, gate, 0, part)
        elif step == 1:
            (
                enc_down_bias, enc_up_bias, enc_up, enc_down,
                post_gain, post_shift, proj_weight, proj_bias, rms_gain, slot_source, block,
            ) = stage(
                (
                    enc_down_bias, enc_up_bias, enc_up, enc_down,
                    post_gain, post_shift, proj_weight, proj_bias, rms_gain, slot_source,
                ),
                block,
                after=(prompts, proj_pair, proj_bias_pair),
            )
        block = jnp.concatenate([block, arrived])
    total, base = encoder(
        block,
        (enc_gain, enc_shift, enc_down_bias, enc_up_bias, bias_pair),
        (enc_up, up_pair),
        (enc_down, down_pair),
        bits,
    )
    arrived = None
    for step, bit in enumerate((steps[1], steps[0], *steps[2:])):
        if arrived is not None:
            total = total + arrived.astype(jnp.float32)
        outgoing = total.astype(jnp.bfloat16)
        if step != 1:
            outgoing, prompts = lax.optimization_barrier((outgoing, prompts))
        arrived = swap(outgoing, bit, count)
        if step != 1:
            early = prompts
            prompts = jnp.concatenate([prompts, swap(prompts, bit, count)])
        if step == 1:
            gate, total = fetch(total, total, gate_rows, gate, 2 * part, 2 * part)
        elif step < 3:
            up, total = fetch(total, total, up_rows, up, step // 2 * large, large)
    post = post_norm(total, arrived, base, post_gain, post_shift, early)
    features = project(post, (proj_weight, proj_pair), (proj_bias, proj_bias_pair))
    for step, bit in enumerate(steps):
        arrived = swap(features, bit, count)
        if step == 1:
            left = width - 2 * large
            up, features = fetch(features, features, up_rows, up, 2 * large, left)
        elif step == 0:
            down, features = fetch(features, features, down_weight, down, 0, 2 * part)
        elif step == 2:
            gate, features = fetch(features, prompts, gate_rows, gate, part, part)
        features = jnp.concatenate([features, arrived])
    features = features, swap(features, 0, count)
    prompts = prompts, swap(prompts, 0, count)
    send, total = language(features, slot_source, prompts, rms_gain, gate, up, down, down_weight, bits)
    total = total + swap(send, 0, count).astype(jnp.float32)
    for bit in range(1, bits):
        half = total.shape[0] // 2
        arrived = swap(total[half:].astype(jnp.bfloat16), bit, count)
        total = total[:half] + arrived.astype(jnp.float32)
    return total.astype(jnp.bfloat16)


def any_shards(*arrays):
    count = lax.axis_size("tp")
    bits = count.bit_length() - 1
    whole_tiles = (
        arrays[9].shape[1] % 128 == 0
        and arrays[3].shape[0] % 16 == 0
        and arrays[16].shape[0] % 16 == 0
    )
    if count == 1 << bits and bits > 3 and whole_tiles:
        return fused_shards(bits, *arrays)
    return shards(*arrays)


def solution(mesh):
    placed = (
        P(("groups", "tp"), None),
        P(),
        P(),
        P("tp", None),
        P("tp"),
        P("tp", None),
        P(),
        P(),
        P(),
        P(None, "tp"),
        P("tp"),
        P("groups"),
        P(("groups", "tp"), None),
        P(),
        P(None, "tp"),
        P(None, "tp"),
        P("tp", None),
    )
    return jax.shard_map(
        any_shards, mesh=mesh, in_specs=placed, out_specs=P(("groups", "tp"), None), check_vma=False
    )
```

```python
import functools

import jax
import jax.numpy as jnp
from jax import lax
from jax.experimental import pallas as pl
from jax.experimental.pallas import tpu as pltpu
from jax.sharding import PartitionSpec as P


def mask_of(bit):
    return (1 << bit) | 1 if bit else 1


def parity_of(index, bits):
    parity = index
    for bit in range(1, bits):
        parity = parity ^ (index >> bit)
    return parity & 1


def exchanged(flags, odd):
    differ = (flags[1] ^ flags[2]) & odd
    return [flags[0], flags[1] ^ differ, flags[2] ^ differ, *flags[3:]]


def slot_of(offset, bits, parity):
    across = parity_of(offset, bits)
    flags = exchanged([(offset >> bit) & 1 for bit in range(bits)], parity ^ across)
    slot = across << (bits - 1)
    for bit in range(1, bits):
        slot = slot + (flags[bit] << (bits - 1 - bit))
    return slot


def offset_of(slot, bits, parity):
    across = (slot >> (bits - 1)) & 1
    flags = [(slot >> (bits - 1 - bit)) & 1 for bit in range(bits)]
    flags = exchanged(flags, parity ^ across)
    offset = across
    for bit in range(1, bits):
        offset = offset ^ (flags[bit] * mask_of(bit))
    return offset


def swap(value, bit, count):
    bits = count.bit_length() - 1
    pairs = []
    for i in range(count):
        across = 3 - bit if bit in (1, 2) and parity_of(i, bits) else bit
        pairs.append((i, i ^ mask_of(across)))
    return lax.ppermute(value, "tp", pairs)


def in_hbm(value):
    return pltpu.with_memory_space_constraint(value, pltpu.HBM)


def row(ref, part=slice(None)):
    return ref[part].reshape(1, -1)


def dot_last(left, right):
    return lax.dot_general(
        left, right, (((1,), (1,)), ((), ())), preferred_element_type=jnp.float32
    )


def group_device(place, parity, bits):
    return 2 * place + (parity ^ parity_of(place, bits))


def encoder_kernel(
    bits, frames, gain, shift, down_bias, bias, bias_pair, up, up_pair, down, down_pair,
    sums, base,
):
    me = lax.axis_index("tp")
    rows = frames.shape[0]
    pooled = rows // 2
    own = rows >> (bits - 1)
    out_row = lax.broadcasted_iota(jnp.int32, (rows, rows), 0)
    in_row = lax.broadcasted_iota(jnp.int32, (rows, rows), 1)
    frame = jnp.where(out_row < pooled, 2 * out_row, 2 * (out_row - pooled) + 1)
    device = group_device(frame // own, parity_of(me, bits), bits)
    place = slot_of(device ^ me, bits, parity_of(me, bits)) * own + frame % own
    order = jnp.where(place == in_row, 1.0, 0.0).astype(jnp.bfloat16)
    values = jnp.dot(order, frames[...], preferred_element_type=jnp.float32)
    center = values - jnp.mean(values, axis=-1, keepdims=True)
    spread = jnp.mean(center * center, axis=-1, keepdims=True)
    base[...] = (values[:pooled] + values[pooled:]) * 0.5 + row(down_bias)
    normed = (center * lax.rsqrt(spread + 1e-05) * row(gain) + row(shift)).astype(jnp.bfloat16)
    result = 0.0
    for weight, offset, back in ((up, bias, down), (up_pair, bias_pair, down_pair)):
        pre_act = dot_last(normed, weight[...]) + row(offset).astype(jnp.float32)
        hidden = 0.5 * pre_act * (1.0 + lax.erf(pre_act * 0.7071067811865476))
        result += jnp.dot(
            hidden.astype(jnp.bfloat16), back[...], preferred_element_type=jnp.float32
        )
    sums[...] = (result[:pooled] + result[pooled:]) * 0.5


def encoder(frames, vectors, ups, downs, bits):
    rows, width = frames.shape
    vmem = pl.BlockSpec(memory_space=pltpu.VMEM)
    return pl.pallas_call(
        functools.partial(encoder_kernel, bits),
        out_shape=[jax.ShapeDtypeStruct((rows // 2, width), jnp.float32)] * 2,
        in_specs=[vmem] * 10,
        out_specs=[vmem] * 2,
        compiler_params=pltpu.CompilerParams(vmem_limit_bytes=8 * 2**20),
        cost_estimate=pl.CostEstimate(
            flops=8 * rows * ups[0].size, bytes_accessed=8 * ups[0].size, transcendentals=0
        ),
    )(frames, *vectors, *ups, *downs)


def post_kernel(total, arrived, base, gain, shift, after, post):
    values = total[...] + arrived[...].astype(jnp.float32) + base[...]
    center = values - jnp.mean(values, axis=-1, keepdims=True)
    spread = jnp.mean(center * center, axis=-1, keepdims=True)
    normed = center * lax.rsqrt(spread + 1e-05) * row(gain) + row(shift)
    post[...] = normed.astype(post.dtype)


def post_norm(total, arrived, base, gain, shift, after):
    vmem = pl.BlockSpec(memory_space=pltpu.VMEM)
    return pl.pallas_call(
        post_kernel,
        out_shape=jax.ShapeDtypeStruct(total.shape, jnp.bfloat16),
        in_specs=[vmem] * 5 + [pl.BlockSpec(memory_space=pl.ANY)],
        out_specs=vmem,
        compiler_params=pltpu.CompilerParams(vmem_limit_bytes=4 * 2**20),
    )(total, arrived, base, gain, shift, after)


def project_kernel(post, weight, weight_pair, bias, bias_pair, out):
    for i, (shard, offset) in enumerate(((weight, bias), (weight_pair, bias_pair))):
        result = jnp.dot(post[...], shard[...], preferred_element_type=jnp.float32)
        out[0, i] = (result + row(offset)).astype(out.dtype)


def project(post, weights, biases):
    vmem = pl.BlockSpec(memory_space=pltpu.VMEM)
    return pl.pallas_call(
        project_kernel,
        out_shape=jax.ShapeDtypeStruct(
            (1, 2, post.shape[0], weights[0].shape[1]), jnp.bfloat16
        ),
        in_specs=[vmem] * 5,
        out_specs=vmem,
        compiler_params=pltpu.CompilerParams(vmem_limit_bytes=4 * 2**20),
    )(post, *weights, *biases)


def stage_kernel(count, extra, carry, *refs):
    sources, sems = refs[:count], refs[-1]
    targets = refs[count + extra + carry :][:count]
    copies = [
        pltpu.make_async_copy(source, target, sems.at[i])
        for i, (source, target) in enumerate(zip(sources, targets))
    ]
    for copy in copies:
        copy.start()
    if carry:
        refs[-2][...] = refs[count][...]
    for copy in copies:
        copy.wait()


def stage(values, *carried, after=()):
    count, carry = len(values), len(carried)
    vmem = pl.BlockSpec(memory_space=pltpu.VMEM)
    return pl.pallas_call(
        functools.partial(stage_kernel, count, len(after), carry),
        out_shape=[pltpu.VMEM(value.shape, value.dtype) for value in values]
        + [jax.ShapeDtypeStruct(value.shape, value.dtype) for value in carried],
        in_specs=[pl.BlockSpec(memory_space=pltpu.HBM)] * count
        + [vmem] * carry
        + [pl.BlockSpec(memory_space=pl.ANY)] * len(after),
        out_specs=[vmem] * (count + carry),
        scratch_shapes=[pltpu.SemaphoreType.DMA((count,))],
        compiler_params=pltpu.CompilerParams(vmem_limit_bytes=2 * 2**20),
        cost_estimate=pl.CostEstimate(
            flops=0, bytes_accessed=2 * sum(value.size for value in values), transcendentals=0
        ),
    )(*[in_hbm(value) for value in values], *carried, *after)


def fetch_kernel(start, width, carried, after, source, *refs):
    target, passed, sem = refs[-3:]
    part = (slice(None), pl.ds(start, width))
    copy = pltpu.make_async_copy(source.at[part], target.at[part], sem)
    copy.start()
    passed[...] = carried[...]
    copy.wait()


def fetch(carried, after, weight, held, start, width):
    vmem = pl.BlockSpec(memory_space=pltpu.VMEM)
    held = [] if held is None else [held]
    return pl.pallas_call(
        functools.partial(fetch_kernel, start, width),
        out_shape=[
            pltpu.VMEM(weight.shape, weight.dtype),
            jax.ShapeDtypeStruct(carried.shape, carried.dtype),
        ],
        in_specs=[
            vmem,
            pl.BlockSpec(memory_space=pl.ANY),
            pl.BlockSpec(memory_space=pltpu.HBM),
        ]
        + [vmem] * len(held),
        out_specs=[vmem] * 2,
        scratch_shapes=[pltpu.SemaphoreType.DMA],
        input_output_aliases={3: 0} if held else {},
        compiler_params=pltpu.CompilerParams(vmem_limit_bytes=2 * 2**20),
        cost_estimate=pl.CostEstimate(
            flops=0, bytes_accessed=2 * weight.shape[0] * width, transcendentals=0
        ),
    )(carried, after, in_hbm(weight), *held)


def language_kernel(
    bits, near, far, source, prompts, others, gain, gate, up, down, down_hbm,
    send, keep, packed, normed, rest, sem,
):
    count, group, columns = 1 << bits, near.shape[2], near.shape[3]
    half, width = prompts.shape
    cut = width // 2
    copy = pltpu.make_async_copy(down_hbm.at[:, pl.ds(cut, cut)], rest, sem)
    copy.start()
    rows = 2 * half
    own = rows >> bits
    me = lax.axis_index("tp")
    out_row = lax.broadcasted_iota(jnp.int32, (rows, rows), 0)
    in_row = lax.broadcasted_iota(jnp.int32, (rows, rows), 1)
    place = (offset_of(out_row // own, bits, parity_of(me, bits)) ^ me) * own + out_row % own
    order = jnp.where(place == in_row, 1.0, 0.0).astype(jnp.bfloat16)
    parity = parity_of(me, bits)
    audio = lax.broadcasted_iota(jnp.int32, (2 * group, rows), 0)
    parities = jnp.where(audio < group, parity, 1 - parity)
    audio = jnp.where(audio < group, audio, audio - group)
    each = group >> (bits - 1)
    wanted = group_device(audio // each, parities, bits) * each + audio % each
    chosen = jnp.where(row(source) == wanted, 1.0, 0.0).astype(jnp.bfloat16)
    pick = dot_last(order, chosen)
    audio_row = jnp.sum(pick, axis=1, keepdims=True) > 0.5
    pick = pick.astype(jnp.bfloat16)
    squares = jnp.zeros((rows, columns), jnp.float32)
    for device in range(count):
        part = slice(device * columns, (device + 1) * columns)
        differs = parity ^ parity_of(device, bits)
        near_slot = slot_of(me ^ device ^ differs, bits, parity)
        far_slot = slot_of(me ^ device ^ differs, bits, 1 - parity)
        piece = jnp.concatenate([near[near_slot, differs], far[far_slot, 1 - differs]])
        found = jnp.dot(pick, piece, preferred_element_type=jnp.float32)
        prompt = jnp.concatenate([prompts[:, part], others[:, part]])
        value = jnp.where(audio_row, found, prompt.astype(jnp.float32))
        squares += value * value
        packed[:, part] = value.astype(jnp.bfloat16)
    scale = lax.rsqrt(jnp.sum(squares, axis=1, keepdims=True) / width + 1e-06)
    for device in range(count):
        part = slice(device * columns, (device + 1) * columns)
        value = packed[:, part].astype(jnp.float32) * scale * row(gain, part)
        normed[:, part] = value.astype(jnp.bfloat16)
    gated, lifted = dot_last(gate[...], normed[...]), dot_last(up[...], normed[...])
    hidden = (gated * jax.nn.sigmoid(gated) * lifted).T.astype(jnp.bfloat16)
    held = lax.broadcasted_iota(jnp.int32, (half, 1), 0) < own
    pieces = 4
    for piece in range(pieces):
        part = slice(piece * width // pieces, (piece + 1) * width // pieces)
        if part.start == cut:
            copy.wait()
        if part.start < cut:
            weight = down[:, part]
        else:
            weight = rest[:, part.start - cut : part.stop - cut]
        result = jnp.dot(hidden, weight, preferred_element_type=jnp.float32)
        send[:, part] = result[half:].astype(jnp.bfloat16)
        keep[:, part] = result[:half] + jnp.where(
            held, packed[:half, part].astype(jnp.float32), 0.0
        )


def language(features, source, prompts, gain, gate, up, down, down_weight, bits):
    half, width = prompts[0].shape
    vmem = pl.BlockSpec(memory_space=pltpu.VMEM)
    return pl.pallas_call(
        functools.partial(language_kernel, bits),
        out_shape=[
            jax.ShapeDtypeStruct((half, width), jnp.bfloat16),
            jax.ShapeDtypeStruct((half, width), jnp.float32),
        ],
        in_specs=[vmem] * 9 + [pl.BlockSpec(memory_space=pltpu.HBM)],
        out_specs=[vmem] * 2,
        scratch_shapes=[pltpu.VMEM((2 * half, width), jnp.bfloat16)] * 2
        + [pltpu.VMEM((down.shape[0], width // 2), down.dtype), pltpu.SemaphoreType.DMA],
        compiler_params=pltpu.CompilerParams(vmem_limit_bytes=12 * 2**20),
        cost_estimate=pl.CostEstimate(
            flops=12 * half * up.size, bytes_accessed=4 * up.size, transcendentals=0
        ),
    )(*features, source, *prompts, gain, gate, up, down, in_hbm(down_weight))


def layer_norm(values, gain, shift):
    center = values - jnp.mean(values, axis=-1, keepdims=True)
    spread = jnp.mean(center * center, axis=-1, keepdims=True)
    return center * lax.rsqrt(spread + 1e-05) * gain + shift


def to_every(piece, count):
    spread = jnp.broadcast_to(piece[None], (count,) + piece.shape)
    return lax.all_to_all(spread, "tp", 0, 0)


def reduce_rows(partial_value, count):
    rows, width = partial_value.shape
    pieces = partial_value.astype(jnp.bfloat16).reshape(count, rows // count, width)
    return jnp.sum(lax.all_to_all(pieces, "tp", 0, 0).astype(jnp.float32), axis=0)


def pool(values):
    paired = values.reshape(values.shape[0] // 2, 2, values.shape[1])
    return (paired[:, 0, :] + paired[:, 1, :]) * 0.5


def shards(
    frames,
    enc_gain,
    enc_shift,
    enc_up,
    enc_up_bias,
    enc_down,
    enc_down_bias,
    post_gain,
    post_shift,
    proj_weight,
    proj_bias,
    slot_source,
    prompt_embeds,
    rms_gain,
    gate_weight,
    up_weight,
    down_weight,
):
    count = lax.axis_size("tp")
    me = lax.axis_index("tp")
    gathered = to_every(frames, count).reshape(-1, frames.shape[1])
    prompts = to_every(prompt_embeds, count).reshape(-1, prompt_embeds.shape[1])
    normed = layer_norm(gathered.astype(jnp.float32), enc_gain, enc_shift).astype(jnp.bfloat16)
    pre_act = lax.dot_general(
        normed, enc_up, (((1,), (1,)), ((), ())), preferred_element_type=jnp.float32
    )
    hidden = jax.nn.gelu(pre_act + enc_up_bias.astype(jnp.float32), approximate=False)
    partial_value = jnp.dot(
        hidden.astype(jnp.bfloat16), enc_down, preferred_element_type=jnp.float32
    )
    branch = reduce_rows(pool(partial_value), count)
    pooled = pool(frames.astype(jnp.float32)) + branch + enc_down_bias
    post = layer_norm(pooled, post_gain, post_shift).astype(jnp.bfloat16)
    post_every = to_every(post, count).reshape(-1, post.shape[1])
    projected = (
        jnp.dot(post_every, proj_weight, preferred_element_type=jnp.float32) + proj_bias
    ).astype(jnp.bfloat16)
    features = to_every(projected, count)
    features = jnp.transpose(features, (1, 0, 2)).reshape(projected.shape[0], -1)
    clipped = jnp.maximum(slot_source, 0)
    packed = jnp.where(
        (slot_source >= 0)[:, None], jnp.take(features, clipped, axis=0), prompts
    )
    residual = packed.astype(jnp.float32)
    scale = lax.rsqrt(jnp.mean(residual * residual, axis=-1, keepdims=True) + 1e-06)
    lm_normed = (residual * scale * rms_gain).astype(jnp.bfloat16)
    gate = jnp.dot(lm_normed, gate_weight, preferred_element_type=jnp.float32)
    lifted = jnp.dot(lm_normed, up_weight, preferred_element_type=jnp.float32)
    lm_hidden = (jax.nn.silu(gate) * lifted).astype(jnp.bfloat16)
    summed = reduce_rows(
        jnp.dot(lm_hidden, down_weight, preferred_element_type=jnp.float32), count
    )
    row_count = prompt_embeds.shape[0]
    own = lax.dynamic_slice_in_dim(packed, me * row_count, row_count).astype(jnp.float32)
    return (own + summed).astype(jnp.bfloat16)


def fused_shards(
    bits,
    frames,
    enc_gain,
    enc_shift,
    enc_up,
    enc_up_bias,
    enc_down,
    enc_down_bias,
    post_gain,
    post_shift,
    proj_weight,
    proj_bias,
    slot_source,
    prompt_embeds,
    rms_gain,
    gate_weight,
    up_weight,
    down_weight,
):
    count = 1 << bits
    width = prompt_embeds.shape[1]
    steps = range(bits - 1, 0, -1)
    gate_rows, up_rows = gate_weight.T, up_weight.T
    arrived = swap(frames, bits - 1, count)
    prompts_arrived = swap(prompt_embeds, bits - 1, count)
    up_pair, down_pair, bias_pair, proj_pair, proj_bias_pair = [
        swap(value, 0, count)
        for value in (enc_up, enc_down, enc_up_bias, proj_weight, proj_bias)
    ]
    block, prompts, enc_gain, enc_shift = stage((frames, prompt_embeds, enc_gain, enc_shift))
    gate = up = down = None
    part = width // 4
    large = width // 2 - width // 8
    block = jnp.concatenate([block, arrived])
    prompts = jnp.concatenate([prompts, prompts_arrived])
    for step, bit in enumerate(steps[1:]):
        arrived = swap(block, bit, count)
        if step == 0:
            gate, block = fetch(block, block, gate_rows, gate, 0, part)
        elif step == 1:
            (
                enc_down_bias, enc_up_bias, enc_up, enc_down,
                post_gain, post_shift, proj_weight, proj_bias, rms_gain, slot_source, block,
            ) = stage(
                (
                    enc_down_bias, enc_up_bias, enc_up, enc_down,
                    post_gain, post_shift, proj_weight, proj_bias, rms_gain, slot_source,
                ),
                block,
                after=(prompts, proj_pair, proj_bias_pair),
            )
        block = jnp.concatenate([block, arrived])
    total, base = encoder(
        block,
        (enc_gain, enc_shift, enc_down_bias, enc_up_bias, bias_pair),
        (enc_up, up_pair),
        (enc_down, down_pair),
        bits,
    )
    arrived = None
    for step, bit in enumerate((steps[1], steps[0], *steps[2:])):
        if arrived is not None:
            total = total + arrived.astype(jnp.float32)
        outgoing = total.astype(jnp.bfloat16)
        if step != 1:
            outgoing, prompts = lax.optimization_barrier((outgoing, prompts))
        arrived = swap(outgoing, bit, count)
        if step != 1:
            early = prompts
            prompts = jnp.concatenate([prompts, swap(prompts, bit, count)])
        if step == 1:
            gate, total = fetch(total, total, gate_rows, gate, 2 * part, 2 * part)
        elif step < 3:
            up, total = fetch(total, total, up_rows, up, step // 2 * large, large)
    post = post_norm(total, arrived, base, post_gain, post_shift, early)
    features = project(post, (proj_weight, proj_pair), (proj_bias, proj_bias_pair))
    for step, bit in enumerate(steps):
        arrived = swap(features, bit, count)
        if step == 1:
            left = width - 2 * large
            up, features = fetch(features, features, up_rows, up, 2 * large, left)
        elif step == 0:
            down, features = fetch(features, features, down_weight, down, 0, 2 * part)
        elif step == 2:
            gate, features = fetch(features, prompts, gate_rows, gate, part, part)
        features = jnp.concatenate([features, arrived])
    features = features, swap(features, 0, count)
    prompts = prompts, swap(prompts, 0, count)
    send, total = language(features, slot_source, prompts, rms_gain, gate, up, down, down_weight, bits)
    total = total + swap(send, 0, count).astype(jnp.float32)
    for bit in range(1, bits):
        half = total.shape[0] // 2
        arrived = swap(total[half:].astype(jnp.bfloat16), bit, count)
        total = total[:half] + arrived.astype(jnp.float32)
    return total.astype(jnp.bfloat16)


def any_shards(*arrays):
    count = lax.axis_size("tp")
    bits = count.bit_length() - 1
    whole_tiles = (
        arrays[9].shape[1] % 128 == 0
        and arrays[3].shape[0] % 16 == 0
        and arrays[16].shape[0] % 16 == 0
    )
    if count == 1 << bits and bits > 3 and whole_tiles:
        return fused_shards(bits, *arrays)
    return shards(*arrays)


def solution(mesh):
    placed = (
        P(("groups", "tp"), None),
        P(),
        P(),
        P("tp", None),
        P("tp"),
        P("tp", None),
        P(),
        P(),
        P(),
        P(None, "tp"),
        P("tp"),
        P("groups"),
        P(("groups", "tp"), None),
        P(),
        P(None, "tp"),
        P(None, "tp"),
        P("tp", None),
    )
    return jax.shard_map(
        any_shards, mesh=mesh, in_specs=placed, out_specs=P(("groups", "tp"), None), check_vma=False
    )
```

```python
import functools

import jax
import jax.numpy as jnp
from jax import lax
from jax.experimental import pallas as pl
from jax.experimental.pallas import tpu as pltpu
from jax.sharding import PartitionSpec as P


def mask_of(bit):
    return (1 << bit) | 1 if bit else 1


def parity_of(index, bits):
    parity = index
    for bit in range(1, bits):
        parity = parity ^ (index >> bit)
    return parity & 1


def exchanged(flags, odd):
    differ = (flags[1] ^ flags[2]) & odd
    return [flags[0], flags[1] ^ differ, flags[2] ^ differ, *flags[3:]]


def slot_of(offset, bits, parity):
    across = parity_of(offset, bits)
    flags = exchanged([(offset >> bit) & 1 for bit in range(bits)], parity ^ across)
    slot = across << (bits - 1)
    for bit in range(1, bits):
        slot = slot + (flags[bit] << (bits - 1 - bit))
    return slot


def offset_of(slot, bits, parity):
    across = (slot >> (bits - 1)) & 1
    flags = [(slot >> (bits - 1 - bit)) & 1 for bit in range(bits)]
    flags = exchanged(flags, parity ^ across)
    offset = across
    for bit in range(1, bits):
        offset = offset ^ (flags[bit] * mask_of(bit))
    return offset


def swap(value, bit, count):
    bits = count.bit_length() - 1
    pairs = []
    for i in range(count):
        across = 3 - bit if bit in (1, 2) and parity_of(i, bits) else bit
        pairs.append((i, i ^ mask_of(across)))
    return lax.ppermute(value, "tp", pairs)


def in_hbm(value):
    return pltpu.with_memory_space_constraint(value, pltpu.HBM)


def row(ref, part=slice(None)):
    return ref[part].reshape(1, -1)


def dot_last(left, right):
    return lax.dot_general(
        left, right, (((1,), (1,)), ((), ())), preferred_element_type=jnp.float32
    )


def group_device(place, parity, bits):
    return 2 * place + (parity ^ parity_of(place, bits))


def encoder_kernel(
    bits, frames, gain, shift, down_bias, bias, bias_pair, up, up_pair, down, down_pair,
    sums, base,
):
    me = lax.axis_index("tp")
    rows = frames.shape[0]
    pooled = rows // 2
    own = rows >> (bits - 1)
    out_row = lax.broadcasted_iota(jnp.int32, (rows, rows), 0)
    in_row = lax.broadcasted_iota(jnp.int32, (rows, rows), 1)
    frame = jnp.where(out_row < pooled, 2 * out_row, 2 * (out_row - pooled) + 1)
    device = group_device(frame // own, parity_of(me, bits), bits)
    place = slot_of(device ^ me, bits, parity_of(me, bits)) * own + frame % own
    order = jnp.where(place == in_row, 1.0, 0.0).astype(jnp.bfloat16)
    values = jnp.dot(order, frames[...], preferred_element_type=jnp.float32)
    center = values - jnp.mean(values, axis=-1, keepdims=True)
    spread = jnp.mean(center * center, axis=-1, keepdims=True)
    base[...] = (values[:pooled] + values[pooled:]) * 0.5 + row(down_bias)
    normed = (center * lax.rsqrt(spread + 1e-05) * row(gain) + row(shift)).astype(jnp.bfloat16)
    result = 0.0
    for weight, offset, back in ((up, bias, down), (up_pair, bias_pair, down_pair)):
        pre_act = dot_last(normed, weight[...]) + row(offset).astype(jnp.float32)
        hidden = 0.5 * pre_act * (1.0 + lax.erf(pre_act * 0.7071067811865476))
        result += jnp.dot(
            hidden.astype(jnp.bfloat16), back[...], preferred_element_type=jnp.float32
        )
    sums[...] = (result[:pooled] + result[pooled:]) * 0.5


def encoder(frames, vectors, ups, downs, bits):
    rows, width = frames.shape
    vmem = pl.BlockSpec(memory_space=pltpu.VMEM)
    return pl.pallas_call(
        functools.partial(encoder_kernel, bits),
        out_shape=[jax.ShapeDtypeStruct((rows // 2, width), jnp.float32)] * 2,
        in_specs=[vmem] * 10,
        out_specs=[vmem] * 2,
        compiler_params=pltpu.CompilerParams(vmem_limit_bytes=8 * 2**20),
        cost_estimate=pl.CostEstimate(
            flops=8 * rows * ups[0].size, bytes_accessed=8 * ups[0].size, transcendentals=0
        ),
    )(frames, *vectors, *ups, *downs)


def post_kernel(total, arrived, base, gain, shift, after, post):
    values = total[...] + arrived[...].astype(jnp.float32) + base[...]
    center = values - jnp.mean(values, axis=-1, keepdims=True)
    spread = jnp.mean(center * center, axis=-1, keepdims=True)
    normed = center * lax.rsqrt(spread + 1e-05) * row(gain) + row(shift)
    post[...] = normed.astype(post.dtype)


def post_norm(total, arrived, base, gain, shift, after):
    vmem = pl.BlockSpec(memory_space=pltpu.VMEM)
    return pl.pallas_call(
        post_kernel,
        out_shape=jax.ShapeDtypeStruct(total.shape, jnp.bfloat16),
        in_specs=[vmem] * 5 + [pl.BlockSpec(memory_space=pl.ANY)],
        out_specs=vmem,
        compiler_params=pltpu.CompilerParams(vmem_limit_bytes=4 * 2**20),
    )(total, arrived, base, gain, shift, after)


def project_kernel(post, weight, weight_pair, bias, bias_pair, out):
    for i, (shard, offset) in enumerate(((weight, bias), (weight_pair, bias_pair))):
        result = jnp.dot(post[...], shard[...], preferred_element_type=jnp.float32)
        out[0, i] = (result + row(offset)).astype(out.dtype)


def project(post, weights, biases):
    vmem = pl.BlockSpec(memory_space=pltpu.VMEM)
    return pl.pallas_call(
        project_kernel,
        out_shape=jax.ShapeDtypeStruct(
            (1, 2, post.shape[0], weights[0].shape[1]), jnp.bfloat16
        ),
        in_specs=[vmem] * 5,
        out_specs=vmem,
        compiler_params=pltpu.CompilerParams(vmem_limit_bytes=4 * 2**20),
    )(post, *weights, *biases)


def stage_kernel(count, extra, carry, *refs):
    sources, sems = refs[:count], refs[-1]
    targets = refs[count + extra + carry :][:count]
    copies = [
        pltpu.make_async_copy(source, target, sems.at[i])
        for i, (source, target) in enumerate(zip(sources, targets))
    ]
    for copy in copies:
        copy.start()
    if carry:
        refs[-2][...] = refs[count][...]
    for copy in copies:
        copy.wait()


def stage(values, *carried, after=()):
    count, carry = len(values), len(carried)
    vmem = pl.BlockSpec(memory_space=pltpu.VMEM)
    return pl.pallas_call(
        functools.partial(stage_kernel, count, len(after), carry),
        out_shape=[pltpu.VMEM(value.shape, value.dtype) for value in values]
        + [jax.ShapeDtypeStruct(value.shape, value.dtype) for value in carried],
        in_specs=[pl.BlockSpec(memory_space=pltpu.HBM)] * count
        + [vmem] * carry
        + [pl.BlockSpec(memory_space=pl.ANY)] * len(after),
        out_specs=[vmem] * (count + carry),
        scratch_shapes=[pltpu.SemaphoreType.DMA((count,))],
        compiler_params=pltpu.CompilerParams(vmem_limit_bytes=2 * 2**20),
        cost_estimate=pl.CostEstimate(
            flops=0, bytes_accessed=2 * sum(value.size for value in values), transcendentals=0
        ),
    )(*[in_hbm(value) for value in values], *carried, *after)


def fetch_kernel(start, width, carried, after, source, *refs):
    target, passed, sem = refs[-3:]
    part = (slice(None), pl.ds(start, width))
    copy = pltpu.make_async_copy(source.at[part], target.at[part], sem)
    copy.start()
    passed[...] = carried[...]
    copy.wait()


def fetch(carried, after, weight, held, start, width):
    vmem = pl.BlockSpec(memory_space=pltpu.VMEM)
    held = [] if held is None else [held]
    return pl.pallas_call(
        functools.partial(fetch_kernel, start, width),
        out_shape=[
            pltpu.VMEM(weight.shape, weight.dtype),
            jax.ShapeDtypeStruct(carried.shape, carried.dtype),
        ],
        in_specs=[
            vmem,
            pl.BlockSpec(memory_space=pl.ANY),
            pl.BlockSpec(memory_space=pltpu.HBM),
        ]
        + [vmem] * len(held),
        out_specs=[vmem] * 2,
        scratch_shapes=[pltpu.SemaphoreType.DMA],
        input_output_aliases={3: 0} if held else {},
        compiler_params=pltpu.CompilerParams(vmem_limit_bytes=2 * 2**20),
        cost_estimate=pl.CostEstimate(
            flops=0, bytes_accessed=2 * weight.shape[0] * width, transcendentals=0
        ),
    )(carried, after, in_hbm(weight), *held)


def language_kernel(
    bits, near, far, source, prompts, others, gain, gate, up, down, down_hbm,
    send, keep, packed, normed, rest, sem,
):
    count, group, columns = 1 << bits, near.shape[2], near.shape[3]
    half, width = prompts.shape
    cut = width // 2
    copy = pltpu.make_async_copy(down_hbm.at[:, pl.ds(cut, cut)], rest, sem)
    copy.start()
    rows = 2 * half
    own = rows >> bits
    me = lax.axis_index("tp")
    out_row = lax.broadcasted_iota(jnp.int32, (rows, rows), 0)
    in_row = lax.broadcasted_iota(jnp.int32, (rows, rows), 1)
    place = (offset_of(out_row // own, bits, parity_of(me, bits)) ^ me) * own + out_row % own
    order = jnp.where(place == in_row, 1.0, 0.0).astype(jnp.bfloat16)
    parity = parity_of(me, bits)
    audio = lax.broadcasted_iota(jnp.int32, (2 * group, rows), 0)
    parities = jnp.where(audio < group, parity, 1 - parity)
    audio = jnp.where(audio < group, audio, audio - group)
    each = group >> (bits - 1)
    wanted = group_device(audio // each, parities, bits) * each + audio % each
    chosen = jnp.where(row(source) == wanted, 1.0, 0.0).astype(jnp.bfloat16)
    pick = dot_last(order, chosen)
    audio_row = jnp.sum(pick, axis=1, keepdims=True) > 0.5
    pick = pick.astype(jnp.bfloat16)
    squares = jnp.zeros((rows, columns), jnp.float32)
    for device in range(count):
        part = slice(device * columns, (device + 1) * columns)
        differs = parity ^ parity_of(device, bits)
        near_slot = slot_of(me ^ device ^ differs, bits, parity)
        far_slot = slot_of(me ^ device ^ differs, bits, 1 - parity)
        piece = jnp.concatenate([near[near_slot, differs], far[far_slot, 1 - differs]])
        found = jnp.dot(pick, piece, preferred_element_type=jnp.float32)
        prompt = jnp.concatenate([prompts[:, part], others[:, part]])
        value = jnp.where(audio_row, found, prompt.astype(jnp.float32))
        squares += value * value
        packed[:, part] = value.astype(jnp.bfloat16)
        normed[:, part] = (value * row(gain, part)).astype(jnp.bfloat16)
    scale = lax.rsqrt(jnp.sum(squares, axis=1, keepdims=True) / width + 1e-06)
    scale = jnp.broadcast_to(scale, (rows, 128)).T[:1, :]
    gated, lifted = dot_last(gate[...], normed[...]), dot_last(up[...], normed[...])
    gated, lifted = gated * scale, lifted * scale
    hidden = (gated * jax.nn.sigmoid(gated) * lifted).T.astype(jnp.bfloat16)
    held = lax.broadcasted_iota(jnp.int32, (half, 1), 0) < own
    pieces = 4
    for piece in range(pieces):
        part = slice(piece * width // pieces, (piece + 1) * width // pieces)
        if part.start == cut:
            copy.wait()
        if part.start < cut:
            weight = down[:, part]
        else:
            weight = rest[:, part.start - cut : part.stop - cut]
        result = jnp.dot(hidden, weight, preferred_element_type=jnp.float32)
        send[:, part] = result[half:].astype(jnp.bfloat16)
        keep[:, part] = result[:half] + jnp.where(
            held, packed[:half, part].astype(jnp.float32), 0.0
        )


def language(features, source, prompts, gain, gate, up, down, down_weight, bits):
    half, width = prompts[0].shape
    vmem = pl.BlockSpec(memory_space=pltpu.VMEM)
    return pl.pallas_call(
        functools.partial(language_kernel, bits),
        out_shape=[
            jax.ShapeDtypeStruct((half, width), jnp.bfloat16),
            jax.ShapeDtypeStruct((half, width), jnp.float32),
        ],
        in_specs=[vmem] * 9 + [pl.BlockSpec(memory_space=pltpu.HBM)],
        out_specs=[vmem] * 2,
        scratch_shapes=[pltpu.VMEM((2 * half, width), jnp.bfloat16)] * 2
        + [pltpu.VMEM((down.shape[0], width // 2), down.dtype), pltpu.SemaphoreType.DMA],
        compiler_params=pltpu.CompilerParams(vmem_limit_bytes=12 * 2**20),
        cost_estimate=pl.CostEstimate(
            flops=12 * half * up.size, bytes_accessed=4 * up.size, transcendentals=0
        ),
    )(*features, source, *prompts, gain, gate, up, down, in_hbm(down_weight))


def layer_norm(values, gain, shift):
    center = values - jnp.mean(values, axis=-1, keepdims=True)
    spread = jnp.mean(center * center, axis=-1, keepdims=True)
    return center * lax.rsqrt(spread + 1e-05) * gain + shift


def to_every(piece, count):
    spread = jnp.broadcast_to(piece[None], (count,) + piece.shape)
    return lax.all_to_all(spread, "tp", 0, 0)


def reduce_rows(partial_value, count):
    rows, width = partial_value.shape
    pieces = partial_value.astype(jnp.bfloat16).reshape(count, rows // count, width)
    return jnp.sum(lax.all_to_all(pieces, "tp", 0, 0).astype(jnp.float32), axis=0)


def pool(values):
    paired = values.reshape(values.shape[0] // 2, 2, values.shape[1])
    return (paired[:, 0, :] + paired[:, 1, :]) * 0.5


def shards(
    frames,
    enc_gain,
    enc_shift,
    enc_up,
    enc_up_bias,
    enc_down,
    enc_down_bias,
    post_gain,
    post_shift,
    proj_weight,
    proj_bias,
    slot_source,
    prompt_embeds,
    rms_gain,
    gate_weight,
    up_weight,
    down_weight,
):
    count = lax.axis_size("tp")
    me = lax.axis_index("tp")
    gathered = to_every(frames, count).reshape(-1, frames.shape[1])
    prompts = to_every(prompt_embeds, count).reshape(-1, prompt_embeds.shape[1])
    normed = layer_norm(gathered.astype(jnp.float32), enc_gain, enc_shift).astype(jnp.bfloat16)
    pre_act = lax.dot_general(
        normed, enc_up, (((1,), (1,)), ((), ())), preferred_element_type=jnp.float32
    )
    hidden = jax.nn.gelu(pre_act + enc_up_bias.astype(jnp.float32), approximate=False)
    partial_value = jnp.dot(
        hidden.astype(jnp.bfloat16), enc_down, preferred_element_type=jnp.float32
    )
    branch = reduce_rows(pool(partial_value), count)
    pooled = pool(frames.astype(jnp.float32)) + branch + enc_down_bias
    post = layer_norm(pooled, post_gain, post_shift).astype(jnp.bfloat16)
    post_every = to_every(post, count).reshape(-1, post.shape[1])
    projected = (
        jnp.dot(post_every, proj_weight, preferred_element_type=jnp.float32) + proj_bias
    ).astype(jnp.bfloat16)
    features = to_every(projected, count)
    features = jnp.transpose(features, (1, 0, 2)).reshape(projected.shape[0], -1)
    clipped = jnp.maximum(slot_source, 0)
    packed = jnp.where(
        (slot_source >= 0)[:, None], jnp.take(features, clipped, axis=0), prompts
    )
    residual = packed.astype(jnp.float32)
    scale = lax.rsqrt(jnp.mean(residual * residual, axis=-1, keepdims=True) + 1e-06)
    lm_normed = (residual * scale * rms_gain).astype(jnp.bfloat16)
    gate = jnp.dot(lm_normed, gate_weight, preferred_element_type=jnp.float32)
    lifted = jnp.dot(lm_normed, up_weight, preferred_element_type=jnp.float32)
    lm_hidden = (jax.nn.silu(gate) * lifted).astype(jnp.bfloat16)
    summed = reduce_rows(
        jnp.dot(lm_hidden, down_weight, preferred_element_type=jnp.float32), count
    )
    row_count = prompt_embeds.shape[0]
    own = lax.dynamic_slice_in_dim(packed, me * row_count, row_count).astype(jnp.float32)
    return (own + summed).astype(jnp.bfloat16)


def fused_shards(
    bits,
    frames,
    enc_gain,
    enc_shift,
    enc_up,
    enc_up_bias,
    enc_down,
    enc_down_bias,
    post_gain,
    post_shift,
    proj_weight,
    proj_bias,
    slot_source,
    prompt_embeds,
    rms_gain,
    gate_weight,
    up_weight,
    down_weight,
):
    count = 1 << bits
    width = prompt_embeds.shape[1]
    steps = range(bits - 1, 0, -1)
    gate_rows, up_rows = gate_weight.T, up_weight.T
    arrived = swap(frames, bits - 1, count)
    prompts_arrived = swap(prompt_embeds, bits - 1, count)
    up_pair, down_pair, bias_pair, proj_pair, proj_bias_pair = [
        swap(value, 0, count)
        for value in (enc_up, enc_down, enc_up_bias, proj_weight, proj_bias)
    ]
    block, prompts, enc_gain, enc_shift = stage((frames, prompt_embeds, enc_gain, enc_shift))
    gate = up = down = None
    part = width // 4
    large = width // 2 - width // 8
    block = jnp.concatenate([block, arrived])
    prompts = jnp.concatenate([prompts, prompts_arrived])
    for step, bit in enumerate(steps[1:]):
        arrived = swap(block, bit, count)
        if step == 0:
            gate, block = fetch(block, block, gate_rows, gate, 0, part)
        elif step == 1:
            (
                enc_down_bias, enc_up_bias, enc_up, enc_down,
                post_gain, post_shift, proj_weight, proj_bias, rms_gain, slot_source, block,
            ) = stage(
                (
                    enc_down_bias, enc_up_bias, enc_up, enc_down,
                    post_gain, post_shift, proj_weight, proj_bias, rms_gain, slot_source,
                ),
                block,
                after=(prompts, proj_pair, proj_bias_pair),
            )
        block = jnp.concatenate([block, arrived])
    total, base = encoder(
        block,
        (enc_gain, enc_shift, enc_down_bias, enc_up_bias, bias_pair),
        (enc_up, up_pair),
        (enc_down, down_pair),
        bits,
    )
    arrived = None
    for step, bit in enumerate((steps[1], steps[0], *steps[2:])):
        if arrived is not None:
            total = total + arrived.astype(jnp.float32)
        outgoing = total.astype(jnp.bfloat16)
        if step != 1:
            outgoing, prompts = lax.optimization_barrier((outgoing, prompts))
        arrived = swap(outgoing, bit, count)
        if step != 1:
            early = prompts
            prompts = jnp.concatenate([prompts, swap(prompts, bit, count)])
        if step == 1:
            gate, total = fetch(total, total, gate_rows, gate, 2 * part, 2 * part)
        elif step < 3:
            up, total = fetch(total, total, up_rows, up, step // 2 * large, large)
    post = post_norm(total, arrived, base, post_gain, post_shift, early)
    features = project(post, (proj_weight, proj_pair), (proj_bias, proj_bias_pair))
    for step, bit in enumerate(steps):
        arrived = swap(features, bit, count)
        if step == 1:
            left = width - 2 * large
            up, features = fetch(features, features, up_rows, up, 2 * large, left)
        elif step == 0:
            down, features = fetch(features, features, down_weight, down, 0, 2 * part)
        elif step == 2:
            gate, features = fetch(features, prompts, gate_rows, gate, part, part)
        features = jnp.concatenate([features, arrived])
    features = features, swap(features, 0, count)
    prompts = prompts, swap(prompts, 0, count)
    send, total = language(features, slot_source, prompts, rms_gain, gate, up, down, down_weight, bits)
    total = total + swap(send, 0, count).astype(jnp.float32)
    for bit in range(1, bits):
        half = total.shape[0] // 2
        arrived = swap(total[half:].astype(jnp.bfloat16), bit, count)
        total = total[:half] + arrived.astype(jnp.float32)
    return total.astype(jnp.bfloat16)


def any_shards(*arrays):
    count = lax.axis_size("tp")
    bits = count.bit_length() - 1
    whole_tiles = (
        arrays[9].shape[1] % 128 == 0
        and arrays[3].shape[0] % 16 == 0
        and arrays[16].shape[0] % 16 == 0
    )
    if count == 1 << bits and bits > 3 and whole_tiles:
        return fused_shards(bits, *arrays)
    return shards(*arrays)


def solution(mesh):
    placed = (
        P(("groups", "tp"), None),
        P(),
        P(),
        P("tp", None),
        P("tp"),
        P("tp", None),
        P(),
        P(),
        P(),
        P(None, "tp"),
        P("tp"),
        P("groups"),
        P(("groups", "tp"), None),
        P(),
        P(None, "tp"),
        P(None, "tp"),
        P("tp", None),
    )
    return jax.shard_map(
        any_shards, mesh=mesh, in_specs=placed, out_specs=P(("groups", "tp"), None), check_vma=False
    )
```
